128 devices in a mesh: replica: 2 (over z_hi), fsdp: 64 (over x, y, z_lo, core).
Axes of the slice: x: 4, y: 4, z: 4 (z_hi: 2, z_lo: 2; z = z_hi * 2 + z_lo), core: 2. Of those that a mesh axis runs over, the one named last changes fastest.
Arguments:
- inputs: bfloat16 [2, 256, 4096], P('replica'), may hold values from -6 to 6
- cotangent: bfloat16 [2, 256, 4096], P('replica', 'fsdp'), may hold values from -6 to 6
- up_weight: bfloat16 [2, 4096, 32768], P('replica', None, 'fsdp'), may hold values from -0.09375 to 0.09375
- down_weight: bfloat16 [2, 32768, 4096], P('replica', 'fsdp'), may hold values from -0.03125 to 0.03125
- local_params: float32 [2, 16, 1048576], P('replica', None, 'fsdp'), may hold values from -6 to 6
- global_params: float32 [16, 1048576], P(None, 'fsdp'), may hold values from -6 to 6
- outer_momentum: float32 [16, 1048576], P(None, 'fsdp'), may hold values from -3 to 3
- plan: int32 [16], replicated, may hold values from 0 to 7, as said below
- fragment_id: int32 [1], replicated, may hold values from 0 to 7
Outputs:
- block_out: bfloat16 [2, 256, 4096], P('replica', 'fsdp')
- input_grad: bfloat16 [2, 256, 4096], P('replica', 'fsdp')
- up_grad: bfloat16 [2, 4096, 32768], P('replica', None, 'fsdp')
- down_grad: bfloat16 [2, 32768, 4096], P('replica', 'fsdp')
- new_global: float32 [16, 1048576], P(None, 'fsdp')
- new_momentum: float32 [16, 1048576], P(None, 'fsdp')
- merged_local: float32 [2, 16, 1048576], P('replica', None, 'fsdp')
The draws below stay inside these ranges and needn't reach their ends.
Inputs may be any that keep to these rules, and one draw needn't show every extreme that they name: `plan`: each of the 8 fragments holds exactly 2 layers.
All inputs are finite; a program needn't handle non-finite values.
Results may differ from the reference program's by a relative error of at most 0.005.
Values may be sent and summed in bfloat16 or wider, within the bound.
A program may use at most 128 MiB of HBM per device.

```python
import jax
import jax.numpy as jnp

D = 4096
FF = 32768
TOKENS = 256
LAYERS = 16
NFRAG = 8
REPLICAS = 2
ENTRIES = 1048576


def draw_plan(key, part):
    key = jax.random.fold_in(key, 7)
    order = jax.random.permutation(key, LAYERS)
    return (order % NFRAG).astype(jnp.int32)


def shard_levels(stream_key, dims, pieces, smallest, high):
    def one(dim, parts):
        heights = jax.random.uniform(jax.random.fold_in(jax.random.fold_in(stream_key, 6), dim), (parts,), jnp.float32, smallest / len(pieces), high / len(pieces))
        return jnp.repeat(jnp.exp(heights), dims[dim] // parts).reshape((-1,) + (1,) * (len(dims) - dim - 1))

    level = one(*pieces[0])
    for cut in pieces[1:]:
        level = level * one(*cut)
    return level


def normal_values(stream_key, shape, width, reach, shards=(), dtype=jnp.bfloat16):
    factor_of = shard_levels(stream_key, shape, shards, -0.22, 0.18) if shards else 1.0
    array = jax.random.normal(stream_key, shape, jnp.float32) * width * factor_of
    return jnp.minimum(jnp.maximum(array, -reach), reach).astype(dtype)


def setup_inputs(seed: int = 0) -> dict:
    key_of = jax.random.split(jax.random.key(seed), 10)
    return {
        "inputs": normal_values(key_of[0], (REPLICAS, TOKENS, D), 1.0, 6.0, ((0, 2),)),
        "cotangent": normal_values(key_of[1], (REPLICAS, TOKENS, D), 1.0, 6.0, ((0, 2), (1, 64))),
        "up_weight": normal_values(key_of[2], (REPLICAS, D, FF), D ** -0.5, 0.09375, ((0, 2), (2, 64))),
        "down_weight": normal_values(key_of[3], (REPLICAS, FF, D), FF ** -0.5, 0.03125, ((0, 2), (1, 64))),
        "local_params": normal_values(key_of[4], (REPLICAS, LAYERS, ENTRIES), 1.0, 6.0, ((0, 2), (2, 64)), jnp.float32),
        "global_params": normal_values(key_of[5], (LAYERS, ENTRIES), 1.0, 6.0, ((1, 64),), jnp.float32),
        "outer_momentum": normal_values(key_of[6], (LAYERS, ENTRIES), 0.5, 3.0, ((1, 64),), jnp.float32),
        "plan": draw_plan(jax.random.fold_in(key_of[9], 71), 0),
        "fragment_id": jax.random.randint(key_of[8], (1,), 0, NFRAG).astype(jnp.int32),
    }


def gelu_value(u):
    t = jnp.tanh(0.7978845608 * (u + 0.044715 * u * u * u))
    return 0.5 * u * (1.0 + t)


def gelu_slope(u):
    t = jnp.tanh(0.7978845608 * (u + 0.044715 * u * u * u))
    return 0.5 * (1.0 + t) + 0.5 * u * (1.0 - t * t) * 0.7978845608 * (1.0 + 3.0 * 0.044715 * u * u)


def reference(inputs, cotangent, up_weight, down_weight, local_params, global_params, outer_momentum, plan, fragment_id):
    outs_y, outs_dx, outs_gu, outs_gd = [], [], [], []
    for r in range(REPLICAS):
        x = inputs[r]
        dy = cotangent[r]
        pre = jnp.dot(x, up_weight[r], preferred_element_type=jnp.float32)
        hidden = gelu_value(pre).astype(jnp.bfloat16)
        outs_y.append(jnp.dot(hidden, down_weight[r], preferred_element_type=jnp.float32).astype(jnp.bfloat16))
        hidden_grad = jnp.dot(dy, down_weight[r].T, preferred_element_type=jnp.float32)
        pre_grad = (hidden_grad * gelu_slope(pre)).astype(jnp.bfloat16)
        outs_gd.append(jnp.dot(hidden.T, dy, preferred_element_type=jnp.float32).astype(jnp.bfloat16))
        outs_gu.append(jnp.dot(x.T, pre_grad, preferred_element_type=jnp.float32).astype(jnp.bfloat16))
        outs_dx.append(jnp.dot(pre_grad, up_weight[r].T, preferred_element_type=jnp.float32).astype(jnp.bfloat16))
    selected = (plan == fragment_id[0])[:, None]
    total = local_params[0]
    for r in range(1, REPLICAS):
        total = total + local_params[r]
    delta = global_params - total / REPLICAS
    momentum = 0.9 * outer_momentum + delta
    updated = global_params - 0.7 * (delta + 0.9 * momentum)
    new_momentum = jnp.where(selected, momentum, outer_momentum)
    new_global = jnp.where(selected, updated, global_params)
    merged_local = jnp.where(selected[None], 0.5 * local_params + 0.5 * new_global[None], local_params)
    return (jnp.stack(outs_y), jnp.stack(outs_dx), jnp.stack(outs_gu), jnp.stack(outs_gd), new_global, new_momentum, merged_local)
```

```python
import jax
import jax.numpy as jnp
from jax import lax
from jax.experimental import pallas as pl
from jax.experimental.pallas import tpu as pltpu
from jax.sharding import PartitionSpec as P

BF = jnp.bfloat16
F32 = jnp.float32
MESH = pl.DeviceIdType.MESH
HALF = 2048


def dot(a, b, ca, cb):
    return lax.dot_general(a, b, (((ca,), (cb,)), ((), ())), preferred_element_type=F32)


def selected_rows(plan_ref, frag_ref):
    first, last = jnp.int32(15), jnp.int32(0)
    for layer in range(16):
        hit = plan_ref[layer] == frag_ref[0]
        first = jnp.minimum(first, jnp.where(hit, layer, 15))
        last = jnp.maximum(last, jnp.where(hit, layer, 0))
    return first, last


def step_kernel(
    x_hbm, cot_hbm, wu_hbm, wd_hbm, lp_hbm, plan_ref, frag_ref,
    bo_ref, ig_ref, cot_out, hid_out, pg_out, prow_ref,
    x_v, wu, wd, lp, cot4, st, cotg, slope, hid, pg, msg, peer_msg,
    own, sb, rb, part, r1, sp, rp,
    lsem, osem, s1, q1, s3, q3, s4, q4, s0, q0, sr, qr, s2, q2, sx, qx,
):
    rep = lax.axis_index("replica")
    f = lax.axis_index("fsdp")
    x, y, z, c = f // 16, (f // 4) % 4, (f // 2) % 2, f % 2
    other = 1 - c
    lo = pl.multiple_of(c * HALF, HALF)
    hi = pl.multiple_of(other * HALF, HALF)
    ring = jnp.where(c == 0, x, y)
    plane = jnp.where(c == 0, y, x)

    def dev(xx, yy, zz, cc):
        return (rep, ((xx * 4 + yy) * 2 + zz) * 2 + cc)

    def on_ring(r):
        return (rep, jnp.where(c == 0, ((r * 4 + y) * 2 + z) * 2 + c, ((x * 4 + r) * 2 + z) * 2 + c))

    def remote(src, dst, ssem, rsem, device):
        return pltpu.make_async_remote_copy(
            src_ref=src, dst_ref=dst, send_sem=ssem, recv_sem=rsem, device_id=device, device_id_type=MESH
        )

    loads = [
        pltpu.make_async_copy(cot_hbm.at[0], cot4, lsem.at[0]),
        pltpu.make_async_copy(x_hbm.at[0], x_v, lsem.at[1]),
        pltpu.make_async_copy(wu_hbm.at[0], wu, lsem.at[2]),
        pltpu.make_async_copy(wd_hbm.at[0], wd, lsem.at[3]),
        pltpu.make_async_copy(lp_hbm.at[0], lp, lsem.at[4]),
    ]
    for load in loads:
        load.start()

    barrier = pltpu.get_barrier_semaphore()

    def greet(k, _):
        u, zz, cc = k // 4, (k // 2) % 2, k % 2

        @pl.when((u * 16 + y * 4 + zz * 2 + cc) != f)
        def _():
            pl.semaphore_signal(barrier, inc=1, device_id=dev(u, y, zz, cc), device_id_type=MESH)

        @pl.when(u != y)
        def _():
            pl.semaphore_signal(barrier, inc=1, device_id=dev(x, u, zz, cc), device_id_type=MESH)

        return 0

    lax.fori_loop(0, 16, greet, 0)
    pl.semaphore_signal(barrier, inc=1, device_id=(1 - rep, f), device_id_type=MESH)
    pl.semaphore_wait(barrier, 28)

    loads[0].wait()
    st[plane * 4 + z * 2 + c] = cot4[:, pl.ds(lo, HALF)]

    def to_core0(k):
        u, zz = k // 2, k % 2
        return remote(cot4.at[:, pl.ds(0, HALF)], st.at[y * 4 + z * 2 + c], s1.at[k], q1.at[y * 4 + z * 2 + c], dev(x, u, zz, 0))

    def to_core1(k):
        u, zz = k // 2, k % 2
        return remote(cot4.at[:, pl.ds(HALF, HALF)], st.at[x * 4 + z * 2 + c], s1.at[8 + k], q1.at[x * 4 + z * 2 + c], dev(u, y, zz, 1))

    def not_self0(k):
        return (c == 1) | (k != y * 2 + z)

    def not_self1(k):
        return (c == 0) | (k != x * 2 + z)

    def stage1(k, _):
        @pl.when(not_self0(k))
        def _():
            to_core0(k).start()

        @pl.when(not_self1(k))
        def _():
            to_core1(k).start()

        return 0

    lax.fori_loop(0, 8, stage1, 0)

    loads[4].wait()
    i0, i1 = selected_rows(plan_ref, frag_ref)
    msg[0:1, :] = lp[pl.ds(i0, 1), :].astype(BF)
    msg[1:2, :] = lp[pl.ds(i1, 1), :].astype(BF)
    swap = remote(msg, peer_msg, sx.at[0], qx.at[0], (1 - rep, f))
    swap.start()

    loads[1].wait()
    loads[2].wait()
    slope[...] = dot(x_v[...], wu[...], 1, 0)
    u = slope[...]
    t = jnp.tanh(0.7978845608 * (u + 0.044715 * u * u * u))
    hid[...] = (0.5 * u * (1.0 + t)).astype(BF)
    slope[...] = 0.5 * (1.0 + t) + 0.5 * u * (1.0 - t * t) * 0.7978845608 * (1.0 + 3.0 * 0.044715 * u * u)

    def arrive1(k, _):
        @pl.when(k != plane * 4 + z * 2 + c)
        def _():
            remote(st.at[k], st.at[k], s1.at[k], q1.at[k], dev(x, y, z, other)).wait_recv()

        return 0

    lax.fori_loop(0, 16, arrive1, 0)
    for q in range(4):
        block = jnp.concatenate([st[4 * q + j].astype(F32) for j in range(4)], axis=0).astype(BF)

        @pl.when(c == 0)
        def _():
            cotg[x, q, :, 0:HALF] = block

        @pl.when(c == 1)
        def _():
            cotg[q, y, :, HALF:] = block

    def slab0(r):
        return cotg.at[r, :, :, pl.ds(0, HALF)]

    def slab1(r):
        return cotg.at[:, r, :, pl.ds(HALF, HALF)]

    def ring_copy(slab, d):
        s = slab(ring)
        return remote(s, s, s3.at[d - 1], q3.at[d - 1], on_ring((ring + d) % 4))

    def core_copy(slab, d):
        s = slab((ring + 4 - d) % 4)
        return remote(s, s, s4.at[d], q4.at[d], dev(x, y, z, other))

    def per_core(fn):
        @pl.when(c == 0)
        def _():
            fn(slab0, slab1)

        @pl.when(c == 1)
        def _():
            fn(slab1, slab0)

    def stage2(mine, theirs):
        for d in (1, 3, 2):
            ring_copy(mine, d).start()
        core_copy(mine, 0).start()

    per_core(stage2)

    def first(n, mine_fn, theirs_fn):
        sb[n] = theirs_fn().astype(BF).reshape(4, 4, 16, HALF)
        remote(sb.at[n], rb.at[n], s0.at[n], q0.at[n], dev(x, y, z, other)).start()
        own[...] = mine_fn()

    def first_done(n):
        remote(sb.at[n], rb.at[n], s0.at[n], q0.at[n], dev(x, y, z, other)).wait_recv()
        part[n] = (own[...].reshape(4, 4, 16, HALF) + rb[n].astype(F32)).astype(BF)

    def second_copy(n, d, core):
        r = (ring + d) % 4
        src = part.at[n, r] if core == 0 else part.at[n, :, r]
        return remote(src, r1.at[n, d - 1], sr.at[n, d - 1], qr.at[n, d - 1], on_ring(r))

    def second(n):
        for core in (0, 1):
            @pl.when(c == core)
            def _():
                for d in (1, 3, 2):
                    second_copy(n, d, core).start()

    def third_copy(n, k):
        q, zz, cc = k // 4, (k // 2) % 2, k % 2
        target = (rep, jnp.where(c == 0, x * 16 + q * 4, q * 16 + y * 4) + zz * 2 + cc)
        slot = c * 8 + plane * 2 + z
        return remote(sp.at[n, k], rp.at[n, slot], s2.at[n, k], q2.at[n, slot], target)

    def second_done(n):
        for d in (1, 3, 2):
            second_copy(n, d, 0).wait_recv()
        for core in (0, 1):
            @pl.when(c == core)
            def _():
                for q in range(4):
                    mine = part[n, x, q] if core == 0 else part[n, q, y]
                    v = mine.astype(F32) + r1[n, 0, q].astype(F32) + r1[n, 1, q].astype(F32) + r1[n, 2, q].astype(F32)
                    for j in range(4):
                        sp[n, 4 * q + j] = v[4 * j : 4 * j + 4].astype(BF)

    def third(n):
        def go(k, _):
            @pl.when(k != plane * 4 + z * 2 + c)
            def _():
                third_copy(n, k).start()

            return 0

        rp[n, c * 8 + plane * 2 + z] = sp[n, plane * 4 + z * 2 + c]
        lax.fori_loop(0, 16, go, 0)

    def third_done(n, out):
        def go(k, _):
            @pl.when(k != c * 8 + plane * 2 + z)
            def _():
                remote(rp.at[n, k], rp.at[n, k], s2.at[n, k], q2.at[n, k], dev(x, y, z, other)).wait_recv()

            return 0

        lax.fori_loop(0, 16, go, 0)
        for h in (0, 1):
            v = rp[n, 8 * h].astype(F32)
            for k in range(1, 8):
                v = v + rp[n, 8 * h + k].astype(F32)
            out[0, :, h * HALF : (h + 1) * HALF] = v.astype(BF)

    loads[3].wait()
    first(
        0,
        lambda: dot(hid[...], wd[:, pl.ds(lo, HALF)], 1, 0),
        lambda: dot(hid[...], wd[:, pl.ds(hi, HALF)], 1, 0),
    )
    first_done(0)

    def stage3(mine, theirs):
        for d in (1, 3, 2):
            ring_copy(mine, d).wait_recv()
            core_copy(mine, d).start()

    per_core(stage3)
    second(0)

    def stage4(mine, theirs):
        for d in range(4):
            s = theirs(0)
            remote(s, s, s4.at[d], q4.at[d], dev(x, y, z, other)).wait_recv()

    per_core(stage4)

    hg = dot(cotg[...].reshape(256, 4096), wd[...], 1, 1)
    pg[...] = (hg * slope[...]).astype(BF)
    first(
        1,
        lambda: dot(pg[...], wu[pl.ds(lo, HALF), :], 1, 1),
        lambda: dot(pg[...], wu[pl.ds(hi, HALF), :], 1, 1),
    )
    first_done(1)
    second(1)

    outs = [
        pltpu.make_async_copy(cotg, cot_out, osem.at[0]),
        pltpu.make_async_copy(hid, hid_out, osem.at[1]),
        pltpu.make_async_copy(pg, pg_out, osem.at[2]),
    ]
    for o in outs:
        o.start()
    swap.wait_recv()
    prow_ref[...] = peer_msg[...].astype(F32)

    second_done(0)
    third(0)
    second_done(1)
    third(1)
    third_done(0, bo_ref)
    third_done(1, ig_ref)

    for o in outs:
        o.wait()
    swap.wait_send()

    def sent1(k, _):
        @pl.when(not_self0(k))
        def _():
            to_core0(k).wait_send()

        @pl.when(not_self1(k))
        def _():
            to_core1(k).wait_send()

        return 0

    lax.fori_loop(0, 8, sent1, 0)

    def sent2(mine, theirs):
        for d in (1, 2, 3):
            ring_copy(mine, d).wait_send()
        for d in range(4):
            core_copy(mine, d).wait_send()

    per_core(sent2)
    for n in (0, 1):
        remote(sb.at[n], rb.at[n], s0.at[n], q0.at[n], dev(x, y, z, other)).wait_send()
        for core in (0, 1):
            @pl.when(c == core)
            def _():
                for d in (1, 2, 3):
                    second_copy(n, d, core).wait_send()

        def sent3(k, _):
            @pl.when(k != plane * 4 + z * 2 + c)
            def _():
                third_copy(n, k).wait_send()

            return 0

        lax.fori_loop(0, 16, sent3, 0)


def step_call(x, cot, wu, wd, lp, plan, frag):
    hbm = pl.BlockSpec(memory_space=pl.ANY)
    smem = pl.BlockSpec(memory_space=pltpu.SMEM)
    vmem = pl.BlockSpec(memory_space=pltpu.VMEM)
    dma = pltpu.SemaphoreType.DMA
    return pl.pallas_call(
        step_kernel,
        out_shape=(
            jax.ShapeDtypeStruct((1, 4, 4096), BF),
            jax.ShapeDtypeStruct((1, 4, 4096), BF),
            jax.ShapeDtypeStruct((4, 4, 16, 4096), BF),
            jax.ShapeDtypeStruct((256, 512), BF),
            jax.ShapeDtypeStruct((256, 512), BF),
            jax.ShapeDtypeStruct((2, 16384), F32),
        ),
        in_specs=[hbm, hbm, hbm, hbm, hbm, smem, smem],
        out_specs=(vmem, vmem, hbm, hbm, hbm, vmem),
        scratch_shapes=[
            pltpu.VMEM((256, 4096), BF),
            pltpu.VMEM((4096, 512), BF),
            pltpu.VMEM((512, 4096), BF),
            pltpu.VMEM((16, 16384), F32),
            pltpu.VMEM((4, 4096), BF),
            pltpu.VMEM((16, 4, HALF), BF),
            pltpu.VMEM((4, 4, 16, 4096), BF),
            pltpu.VMEM((256, 512), F32),
            pltpu.VMEM((256, 512), BF),
            pltpu.VMEM((256, 512), BF),
            pltpu.VMEM((2, 16384), BF),
            pltpu.VMEM((2, 16384), BF),
            pltpu.VMEM((256, HALF), F32),
            pltpu.VMEM((2, 4, 4, 16, HALF), BF),
            pltpu.VMEM((2, 4, 4, 16, HALF), BF),
            pltpu.VMEM((2, 4, 4, 16, HALF), BF),
            pltpu.VMEM((2, 3, 4, 16, HALF), BF),
            pltpu.VMEM((2, 16, 4, HALF), BF),
            pltpu.VMEM((2, 16, 4, HALF), BF),
            dma((5,)), dma((3,)),
            dma((16,)), dma((16,)),
            dma((3,)), dma((3,)),
            dma((4,)), dma((4,)),
            dma((2,)), dma((2,)),
            dma((2, 3)), dma((2, 3)),
            dma((2, 16)), dma((2, 16)),
            dma((1,)), dma((1,)),
        ],
        compiler_params=pltpu.CompilerParams(collective_id=1, has_side_effects=True, vmem_limit_bytes=56 << 20),
        cost_estimate=pl.CostEstimate(flops=4 * 2 * 256 * 4096 * 512, bytes_accessed=14 << 20, transcendentals=1 << 17),
    )(x, cot, wu, wd, lp, plan, frag)


def update_kernel(
    plan_ref, frag_ref, bo_in, ig_in, x_ref, cot_ref, hid_ref, pg_ref, lp_ref, gp_ref, om_ref, prow_ref,
    bo_ref, ig_ref, ug_ref, dg_ref, ng_ref, nm_ref, ml_ref,
):
    @pl.when(pl.program_id(0) == 0)
    def _():
        bo_ref[...] = bo_in[...]
        ig_ref[...] = ig_in[...]

    dg_ref[0] = dot(hid_ref[...], cot_ref[...], 0, 0).astype(BF)
    ug_ref[0] = dot(x_ref[0], pg_ref[...], 0, 0).astype(BF)
    i0, i1 = selected_rows(plan_ref, frag_ref)
    mine, g, om = lp_ref[0], gp_ref[...], om_ref[...]
    row = lax.broadcasted_iota(jnp.int32, mine.shape, 0)
    keep = (row == i0) | (row == i1)
    peer = jnp.where(row == i0, prow_ref[0:1, :], prow_ref[1:2, :])
    delta = g - (mine.astype(BF).astype(F32) + peer) / 2
    momentum = 0.9 * om + delta
    updated = g - 0.7 * (delta + 0.9 * momentum)
    ng = jnp.where(keep, updated, g)
    nm_ref[...] = jnp.where(keep, momentum, om)
    ng_ref[...] = ng
    ml_ref[0] = jnp.where(keep, 0.5 * mine + 0.5 * ng, mine)


def update_call(plan, frag, bo, ig, x, cot, hid, pg, lp, gp, om, prow):
    steps = 4
    w, e = 4096 // steps, 16384 // steps
    smem = pl.BlockSpec(memory_space=pltpu.SMEM)
    whole3 = pl.BlockSpec((1, 4, 4096), lambda i: (0, 0, 0))
    act = pl.BlockSpec((256, 512), lambda i: (0, 0))
    params = pl.BlockSpec((16, e), lambda i: (0, i))
    params3 = pl.BlockSpec((1, 16, e), lambda i: (0, 0, i))
    return pl.pallas_call(
        update_kernel,
        grid=(steps,),
        out_shape=(
            jax.ShapeDtypeStruct((1, 4, 4096), BF),
            jax.ShapeDtypeStruct((1, 4, 4096), BF),
            jax.ShapeDtypeStruct((1, 4096, 512), BF),
            jax.ShapeDtypeStruct((1, 512, 4096), BF),
            jax.ShapeDtypeStruct((16, 16384), F32),
            jax.ShapeDtypeStruct((16, 16384), F32),
            jax.ShapeDtypeStruct((1, 16, 16384), F32),
        ),
        in_specs=[
            smem, smem, whole3, whole3,
            pl.BlockSpec((1, 256, w), lambda i: (0, 0, i)),
            pl.BlockSpec((256, w), lambda i: (0, i)),
            act, act, params3, params, params,
            pl.BlockSpec((2, e), lambda i: (0, i)),
        ],
        out_specs=(
            whole3, whole3,
            pl.BlockSpec((1, w, 512), lambda i: (0, i, 0)),
            pl.BlockSpec((1, 512, w), lambda i: (0, 0, i)),
            params, params, params3,
        ),
        compiler_params=pltpu.CompilerParams(vmem_limit_bytes=40 << 20),
        cost_estimate=pl.CostEstimate(flops=2 * 2 * 256 * 4096 * 512, bytes_accessed=18 << 20, transcendentals=0),
    )(plan, frag, bo, ig, x, cot, hid, pg, lp, gp, om, prow)


def on_device(inputs, cotangent, up_weight, down_weight, local_params, global_params, outer_momentum, plan, fragment_id):
    bo, ig, cot, hid, pg, prow = step_call(inputs, cotangent, up_weight, down_weight, local_params, plan, fragment_id)
    return update_call(
        plan, fragment_id, bo, ig, inputs, cot.reshape(256, 4096), hid, pg,
        local_params, global_params, outer_momentum, prow,
    )


def solution(mesh):
    placed = (
        P("replica", None, None),
        P("replica", "fsdp", None),
        P("replica", None, "fsdp"),
        P("replica", "fsdp", None),
        P("replica", None, "fsdp"),
        P(None, "fsdp"),
        P(None, "fsdp"),
        P(),
        P(),
    )
    return jax.shard_map(
        on_device,
        mesh=mesh,
        in_specs=placed,
        out_specs=(
            P("replica", "fsdp", None),
            P("replica", "fsdp", None),
            P("replica", None, "fsdp"),
            P("replica", "fsdp", None),
            P(None, "fsdp"),
            P(None, "fsdp"),
            P("replica", None, "fsdp"),
        ),
        check_vma=False,
    )
```

```python
import jax
import jax.numpy as jnp
from jax import lax
from jax.experimental import pallas as pl
from jax.experimental.pallas import tpu as pltpu
from jax.sharding import PartitionSpec as P

BF = jnp.bfloat16
F32 = jnp.float32
MESH = pl.DeviceIdType.MESH
HALF = 2048


def dot(a, b, ca, cb):
    return lax.dot_general(a, b, (((ca,), (cb,)), ((), ())), preferred_element_type=F32)


def selected_rows(plan_ref, frag_ref):
    first, last = jnp.int32(15), jnp.int32(0)
    for layer in range(16):
        hit = plan_ref[layer] == frag_ref[0]
        first = jnp.minimum(first, jnp.where(hit, layer, 15))
        last = jnp.maximum(last, jnp.where(hit, layer, 0))
    return first, last


def step_kernel(
    x_hbm, cot_hbm, wu_hbm, wd_hbm, lp_hbm, gp_hbm, om_hbm, plan_ref, frag_ref,
    bo_ref, ig_ref, ug_ref, dg_ref, ng_ref, nm_ref, ml_ref,
    x_v, wu, wd, lp, gp, om, cot4, st, cotg, slope, hid, pg, msg, peer_msg,
    own, sb, rb, part, r1, sp, rp,
    lsem, s1, q1, s3, q3, s4, q4, s0, q0, sr, qr, s2, q2, sx, qx,
):
    rep = lax.axis_index("replica")
    f = lax.axis_index("fsdp")
    x, y, z, c = f // 16, (f // 4) % 4, (f // 2) % 2, f % 2
    other = 1 - c
    lo = pl.multiple_of(c * HALF, HALF)
    hi = pl.multiple_of(other * HALF, HALF)
    ring = jnp.where(c == 0, x, y)
    plane = jnp.where(c == 0, y, x)

    def dev(xx, yy, zz, cc):
        return (rep, ((xx * 4 + yy) * 2 + zz) * 2 + cc)

    def on_ring(r):
        return (rep, jnp.where(c == 0, ((r * 4 + y) * 2 + z) * 2 + c, ((x * 4 + r) * 2 + z) * 2 + c))

    def remote(src, dst, ssem, rsem, device):
        return pltpu.make_async_remote_copy(
            src_ref=src, dst_ref=dst, send_sem=ssem, recv_sem=rsem, device_id=device, device_id_type=MESH
        )

    barrier = pltpu.get_barrier_semaphore()

    def greet(k, _):
        q, zz, cc = k // 4, (k // 2) % 2, k % 2

        @pl.when(k != plane * 4 + z * 2 + c)
        def _():
            target = (rep, jnp.where(c == 0, x * 16 + q * 4, q * 16 + y * 4) + zz * 2 + cc)
            pl.semaphore_signal(barrier, inc=1, device_id=target, device_id_type=MESH)

        return 0

    lax.fori_loop(0, 16, greet, 0)
    for d in (1, 2, 3):
        pl.semaphore_signal(barrier, inc=1, device_id=on_ring((ring + d) % 4), device_id_type=MESH)
    pl.semaphore_signal(barrier, inc=1, device_id=(1 - rep, f), device_id_type=MESH)

    loads = [
        pltpu.make_async_copy(cot_hbm.at[0], cot4, lsem.at[0]),
        pltpu.make_async_copy(x_hbm.at[0], x_v, lsem.at[1]),
        pltpu.make_async_copy(wu_hbm.at[0], wu, lsem.at[2]),
        pltpu.make_async_copy(wd_hbm.at[0], wd, lsem.at[3]),
        pltpu.make_async_copy(lp_hbm.at[0], lp, lsem.at[4]),
        pltpu.make_async_copy(gp_hbm, gp, lsem.at[5]),
        pltpu.make_async_copy(om_hbm, om, lsem.at[6]),
    ]
    for k in (0, 1, 2, 4, 3, 5, 6):
        loads[k].start()
    pl.semaphore_wait(barrier, 19)

    loads[0].wait()
    st[plane * 4 + z * 2 + c] = cot4[:, pl.ds(lo, HALF)]

    def to_core0(k):
        u, zz = k // 2, k % 2
        return remote(cot4.at[:, pl.ds(0, HALF)], st.at[y * 4 + z * 2 + c], s1.at[k], q1.at[y * 4 + z * 2 + c], dev(x, u, zz, 0))

    def to_core1(k):
        u, zz = k // 2, k % 2
        return remote(cot4.at[:, pl.ds(HALF, HALF)], st.at[x * 4 + z * 2 + c], s1.at[8 + k], q1.at[x * 4 + z * 2 + c], dev(u, y, zz, 1))

    def not_self0(k):
        return (c == 1) | (k != y * 2 + z)

    def not_self1(k):
        return (c == 0) | (k != x * 2 + z)

    def stage1(k, _):
        @pl.when(not_self0(k))
        def _():
            to_core0(k).start()

        @pl.when(not_self1(k))
        def _():
            to_core1(k).start()

        return 0

    lax.fori_loop(0, 8, stage1, 0)

    loads[4].wait()
    i0, i1 = selected_rows(plan_ref, frag_ref)
    msg[0:1, :] = lp[pl.ds(i0, 1), :].astype(BF)
    msg[1:2, :] = lp[pl.ds(i1, 1), :].astype(BF)
    swap = remote(msg, peer_msg, sx.at[0], qx.at[0], (1 - rep, f))
    swap.start()

    loads[1].wait()
    loads[2].wait()
    slope[...] = dot(x_v[...], wu[...], 1, 0)
    u = slope[...]
    t = jnp.tanh(0.7978845608 * (u + 0.044715 * u * u * u))
    hid[...] = (0.5 * u * (1.0 + t)).astype(BF)
    slope[...] = 0.5 * (1.0 + t) + 0.5 * u * (1.0 - t * t) * 0.7978845608 * (1.0 + 3.0 * 0.044715 * u * u)

    def arrive1(k, _):
        @pl.when(k != plane * 4 + z * 2 + c)
        def _():
            remote(st.at[k], st.at[k], s1.at[k], q1.at[k], dev(x, y, z, other)).wait_recv()

        return 0

    lax.fori_loop(0, 16, arrive1, 0)
    for q in range(4):
        block = jnp.concatenate([st[4 * q + j].astype(F32) for j in range(4)], axis=0).astype(BF)

        @pl.when(c == 0)
        def _():
            cotg[x, q, :, 0:HALF] = block

        @pl.when(c == 1)
        def _():
            cotg[q, y, :, HALF:] = block

    def slab0(r):
        return cotg.at[r, :, :, pl.ds(0, HALF)]

    def slab1(r):
        return cotg.at[:, r, :, pl.ds(HALF, HALF)]

    def ring_copy(slab, d):
        s = slab(ring)
        return remote(s, s, s3.at[d - 1], q3.at[d - 1], on_ring((ring + d) % 4))

    def core_copy(slab, d):
        s = slab((ring + 4 - d) % 4)
        return remote(s, s, s4.at[d], q4.at[d], dev(x, y, z, other))

    def per_core(fn):
        @pl.when(c == 0)
        def _():
            fn(slab0, slab1)

        @pl.when(c == 1)
        def _():
            fn(slab1, slab0)

    def stage2(mine, theirs):
        for d in (1, 3, 2):
            ring_copy(mine, d).start()
        core_copy(mine, 0).start()

    per_core(stage2)

    def first(n, mine_fn, theirs_fn):
        sb[n] = theirs_fn().astype(BF).reshape(4, 4, 16, HALF)
        remote(sb.at[n], rb.at[n], s0.at[n], q0.at[n], dev(x, y, z, other)).start()
        own[...] = mine_fn()

    def first_done(n):
        remote(sb.at[n], rb.at[n], s0.at[n], q0.at[n], dev(x, y, z, other)).wait_recv()
        part[n] = (own[...].reshape(4, 4, 16, HALF) + rb[n].astype(F32)).astype(BF)

    def second_copy(n, d, core):
        r = (ring + d) % 4
        src = part.at[n, r] if core == 0 else part.at[n, :, r]
        return remote(src, r1.at[n, d - 1], sr.at[n, d - 1], qr.at[n, d - 1], on_ring(r))

    def second(n):
        for core in (0, 1):
            @pl.when(c == core)
            def _():
                for d in (1, 3, 2):
                    second_copy(n, d, core).start()

    def third_copy(n, k):
        q, zz, cc = k // 4, (k // 2) % 2, k % 2
        target = (rep, jnp.where(c == 0, x * 16 + q * 4, q * 16 + y * 4) + zz * 2 + cc)
        slot = c * 8 + plane * 2 + z
        return remote(sp.at[n, k], rp.at[n, slot], s2.at[n, k], q2.at[n, slot], target)

    def second_done(n):
        for d in (1, 3, 2):
            second_copy(n, d, 0).wait_recv()
        for core in (0, 1):
            @pl.when(c == core)
            def _():
                for q in range(4):
                    mine = part[n, x, q] if core == 0 else part[n, q, y]
                    v = mine.astype(F32) + r1[n, 0, q].astype(F32) + r1[n, 1, q].astype(F32) + r1[n, 2, q].astype(F32)
                    for j in range(4):
                        sp[n, 4 * q + j] = v[4 * j : 4 * j + 4].astype(BF)

    def third(n):
        def go(k, _):
            @pl.when(k != plane * 4 + z * 2 + c)
            def _():
                third_copy(n, k).start()

            return 0

        rp[n, c * 8 + plane * 2 + z] = sp[n, plane * 4 + z * 2 + c]
        lax.fori_loop(0, 16, go, 0)

    def third_done(n, out):
        def go(k, _):
            @pl.when(k != c * 8 + plane * 2 + z)
            def _():
                remote(rp.at[n, k], rp.at[n, k], s2.at[n, k], q2.at[n, k], dev(x, y, z, other)).wait_recv()

            return 0

        lax.fori_loop(0, 16, go, 0)
        for h in (0, 1):
            v = rp[n, 8 * h].astype(F32)
            for k in range(1, 8):
                v = v + rp[n, 8 * h + k].astype(F32)
            out[0, :, h * HALF : (h + 1) * HALF] = v.astype(BF)

    loads[3].wait()
    first(
        0,
        lambda: dot(hid[...], wd[:, pl.ds(lo, HALF)], 1, 0),
        lambda: dot(hid[...], wd[:, pl.ds(hi, HALF)], 1, 0),
    )
    first_done(0)

    def stage3(mine, theirs):
        for d in (1, 3, 2):
            ring_copy(mine, d).wait_recv()
            core_copy(mine, d).start()

    per_core(stage3)
    second(0)

    def stage4(mine, theirs):
        for d in range(4):
            s = theirs(0)
            remote(s, s, s4.at[d], q4.at[d], dev(x, y, z, other)).wait_recv()

    per_core(stage4)

    hg = dot(cotg[...].reshape(256, 4096), wd[...], 1, 1)
    pg[...] = (hg * slope[...]).astype(BF)
    first(
        1,
        lambda: dot(pg[...], wu[pl.ds(lo, HALF), :], 1, 1),
        lambda: dot(pg[...], wu[pl.ds(hi, HALF), :], 1, 1),
    )
    first_done(1)
    second(1)

    second_done(0)
    third(0)

    cot = cotg[...].reshape(256, 4096)
    dg_ref[0] = dot(hid[...], cot, 0, 0).astype(BF)
    ug_ref[0] = dot(x_v[...], pg[...], 0, 0).astype(BF)
    loads[5].wait()
    loads[6].wait()
    swap.wait_recv()
    for e in range(0, 16384, 2048):
        cols = slice(e, e + 2048)
        mine, g, mom = lp[:, cols], gp[:, cols], om[:, cols]
        row = lax.broadcasted_iota(jnp.int32, mine.shape, 0)
        keep = (row == i0) | (row == i1)
        theirs = peer_msg[:, cols].astype(F32)
        peer = jnp.where(row == i0, theirs[0:1, :], theirs[1:2, :])
        delta = g - (mine.astype(BF).astype(F32) + peer) / 2
        momentum = 0.9 * mom + delta
        ng = jnp.where(keep, g - 0.7 * (delta + 0.9 * momentum), g)
        nm_ref[:, cols] = jnp.where(keep, momentum, mom)
        ng_ref[:, cols] = ng
        ml_ref[0, :, cols] = jnp.where(keep, 0.5 * mine + 0.5 * ng, mine)

    third_done(0, bo_ref)
    second_done(1)
    third(1)
    third_done(1, ig_ref)

    swap.wait_send()

    def sent1(k, _):
        @pl.when(not_self0(k))
        def _():
            to_core0(k).wait_send()

        @pl.when(not_self1(k))
        def _():
            to_core1(k).wait_send()

        return 0

    lax.fori_loop(0, 8, sent1, 0)

    def sent2(mine, theirs):
        for d in (1, 2, 3):
            ring_copy(mine, d).wait_send()
        for d in range(4):
            core_copy(mine, d).wait_send()

    per_core(sent2)
    for n in (0, 1):
        remote(sb.at[n], rb.at[n], s0.at[n], q0.at[n], dev(x, y, z, other)).wait_send()
        for core in (0, 1):
            @pl.when(c == core)
            def _():
                for d in (1, 2, 3):
                    second_copy(n, d, core).wait_send()

        def sent3(k, _):
            @pl.when(k != plane * 4 + z * 2 + c)
            def _():
                third_copy(n, k).wait_send()

            return 0

        lax.fori_loop(0, 16, sent3, 0)


def step_call(x, cot, wu, wd, lp, gp, om, plan, frag):
    hbm = pl.BlockSpec(memory_space=pl.ANY)
    smem = pl.BlockSpec(memory_space=pltpu.SMEM)
    vmem = pl.BlockSpec(memory_space=pltpu.VMEM)
    dma = pltpu.SemaphoreType.DMA
    return pl.pallas_call(
        step_kernel,
        out_shape=(
            pltpu.VMEM((1, 4, 4096), BF),
            pltpu.VMEM((1, 4, 4096), BF),
            pltpu.VMEM((1, 4096, 512), BF),
            pltpu.VMEM((1, 512, 4096), BF),
            pltpu.VMEM((16, 16384), F32),
            pltpu.VMEM((16, 16384), F32),
            pltpu.VMEM((1, 16, 16384), F32),
        ),
        in_specs=[hbm] * 7 + [smem, smem],
        out_specs=(vmem,) * 7,
        scratch_shapes=[
            pltpu.VMEM((256, 4096), BF),
            pltpu.VMEM((4096, 512), BF),
            pltpu.VMEM((512, 4096), BF),
            pltpu.VMEM((16, 16384), F32),
            pltpu.VMEM((16, 16384), F32),
            pltpu.VMEM((16, 16384), F32),
            pltpu.VMEM((4, 4096), BF),
            pltpu.VMEM((16, 4, HALF), BF),
            pltpu.VMEM((4, 4, 16, 4096), BF),
            pltpu.VMEM((256, 512), F32),
            pltpu.VMEM((256, 512), BF),
            pltpu.VMEM((256, 512), BF),
            pltpu.VMEM((2, 16384), BF),
            pltpu.VMEM((2, 16384), BF),
            pltpu.VMEM((256, HALF), F32),
            pltpu.VMEM((2, 4, 4, 16, HALF), BF),
            pltpu.VMEM((2, 4, 4, 16, HALF), BF),
            pltpu.VMEM((2, 4, 4, 16, HALF), BF),
            pltpu.VMEM((2, 3, 4, 16, HALF), BF),
            pltpu.VMEM((2, 16, 4, HALF), BF),
            pltpu.VMEM((2, 16, 4, HALF), BF),
            dma((7,)),
            dma((16,)), dma((16,)),
            dma((3,)), dma((3,)),
            dma((4,)), dma((4,)),
            dma((2,)), dma((2,)),
            dma((2, 3)), dma((2, 3)),
            dma((2, 16)), dma((2, 16)),
            dma((1,)), dma((1,)),
        ],
        compiler_params=pltpu.CompilerParams(collective_id=1, has_side_effects=True, vmem_limit_bytes=46 << 20),
        cost_estimate=pl.CostEstimate(flops=6 * 2 * 256 * 4096 * 512, bytes_accessed=14 << 20, transcendentals=1 << 17),
    )(x, cot, wu, wd, lp, gp, om, plan, frag)


def write_kernel(*refs):
    n = len(refs) // 2
    copies = [pltpu.make_async_copy(refs[i], refs[n + i], refs[2 * n].at[i]) for i in range(n)]
    for copy in copies:
        copy.start()
    for copy in copies:
        copy.wait()


def write_call(*arrays):
    n = len(arrays)
    return pl.pallas_call(
        write_kernel,
        out_shape=tuple(jax.ShapeDtypeStruct(a.shape, a.dtype) for a in arrays),
        in_specs=[pl.BlockSpec(memory_space=pltpu.VMEM)] * n,
        out_specs=tuple(pl.BlockSpec(memory_space=pl.ANY) for _ in arrays),
        scratch_shapes=[pltpu.SemaphoreType.DMA((n,))],
        compiler_params=pltpu.CompilerParams(has_side_effects=True, vmem_limit_bytes=16 << 20),
        cost_estimate=pl.CostEstimate(flops=0, bytes_accessed=12 << 20, transcendentals=0),
    )(*arrays)


def on_device(inputs, cotangent, up_weight, down_weight, local_params, global_params, outer_momentum, plan, fragment_id):
    return write_call(
        *step_call(
            inputs, cotangent, up_weight, down_weight, local_params, global_params, outer_momentum, plan, fragment_id
        )
    )


def solution(mesh):
    placed = (
        P("replica", None, None),
        P("replica", "fsdp", None),
        P("replica", None, "fsdp"),
        P("replica", "fsdp", None),
        P("replica", None, "fsdp"),
        P(None, "fsdp"),
        P(None, "fsdp"),
        P(),
        P(),
    )
    return jax.shard_map(
        on_device,
        mesh=mesh,
        in_specs=placed,
        out_specs=(
            P("replica", "fsdp", None),
            P("replica", "fsdp", None),
            P("replica", None, "fsdp"),
            P("replica", "fsdp", None),
            P(None, "fsdp"),
            P(None, "fsdp"),
            P("replica", None, "fsdp"),
        ),
        check_vma=False,
    )
```

```python
import jax
import jax.numpy as jnp
from jax import lax
from jax.experimental import pallas as pl
from jax.experimental.pallas import tpu as pltpu
from jax.sharding import PartitionSpec as P

BF = jnp.bfloat16
F32 = jnp.float32
MESH = pl.DeviceIdType.MESH
HALF = 2048
NEAR = (0, 1, 3, 2)
FAR = (2, 1, 3, 0)
PARTS = 2


def dot(a, b, ca, cb):
    return lax.dot_general(a, b, (((ca,), (cb,)), ((), ())), preferred_element_type=F32)


def selected_rows(plan_ref, frag_ref):
    first, last = jnp.int32(15), jnp.int32(0)
    for layer in range(16):
        hit = plan_ref[layer] == frag_ref[0]
        first = jnp.minimum(first, jnp.where(hit, layer, 15))
        last = jnp.maximum(last, jnp.where(hit, layer, 0))
    return first, last


def step_kernel(
    x_hbm, cot_hbm, wu_hbm, wd_hbm, lp_hbm, gp_hbm, om_hbm, plan_ref, frag_ref,
    bo_ref, ig_ref, ug_ref, dg_ref, ng_ref, nm_ref, ml_ref,
    x_v, wu, wd, lp, gp, om, cot4, st, cotg, slope, hid, pg, msg, peer_msg,
    own, sb, rb, part, r1, sp, rp,
    lsem, s1, q1, s3, q3, s4, q4, s0, q0, sr, qr, s2, q2, sx, qx,
):
    rep = lax.axis_index("replica")
    f = lax.axis_index("fsdp")
    x, y, z, c = f // 16, (f // 4) % 4, (f // 2) % 2, f % 2
    other = 1 - c
    lo = pl.multiple_of(c * HALF, HALF)
    hi = pl.multiple_of(other * HALF, HALF)
    ring = jnp.where(c == 0, x, y)
    plane = jnp.where(c == 0, y, x)

    ring_step = jnp.where(c == 0, 16, 4)
    plane_step = jnp.where(c == 0, 4, 16)
    here = plane * 4 + z * 2 + c
    peer = (rep, f + other - c)

    def on_ring(r):
        return (rep, f + (r - ring) * ring_step)

    def in_plane(k):
        return (rep, ring * ring_step + (k // 4) * plane_step + k % 4)

    def block_of(e):
        return (plane + e) % 4

    def rotate(k, fn):
        lax.fori_loop(1, 16, lambda d, _: (fn((k + d) % 16), 0)[1], 0)

    def remote(src, dst, ssem, rsem, device):
        return pltpu.make_async_remote_copy(
            src_ref=src, dst_ref=dst, send_sem=ssem, recv_sem=rsem, device_id=device, device_id_type=MESH
        )

    barrier = pltpu.get_barrier_semaphore()

    rotate(here, lambda k: pl.semaphore_signal(barrier, inc=1, device_id=in_plane(k), device_id_type=MESH))
    for d in (1, 2, 3):
        pl.semaphore_signal(barrier, inc=1, device_id=on_ring((ring + d) % 4), device_id_type=MESH)
    pl.semaphore_signal(barrier, inc=1, device_id=(1 - rep, f), device_id_type=MESH)

    loads = [
        pltpu.make_async_copy(cot_hbm.at[0], cot4, lsem.at[0]),
        pltpu.make_async_copy(x_hbm.at[0], x_v, lsem.at[1]),
        pltpu.make_async_copy(wu_hbm.at[0], wu, lsem.at[2]),
        pltpu.make_async_copy(wd_hbm.at[0], wd, lsem.at[3]),
        pltpu.make_async_copy(lp_hbm.at[0], lp, lsem.at[4]),
        pltpu.make_async_copy(gp_hbm, gp, lsem.at[5]),
        pltpu.make_async_copy(om_hbm, om, lsem.at[6]),
    ]
    for k in (0, 1, 2, 4, 3, 5, 6):
        loads[k].start()
    pl.semaphore_wait(barrier, 19)

    loads[0].wait()
    st[here] = cot4[:, pl.ds(lo, HALF)]

    def same_core(d):
        k = (plane * 2 + z + d) % 8
        target = ring * ring_step + (k // 2) * plane_step + (k % 2) * 2 + c
        return remote(cot4.at[:, pl.ds(lo, HALF)], st.at[here], s1.at[0], q1.at[plane], (rep, target))

    def other_core(d):
        k = (ring * 2 + z + d) % 8
        target = (k // 2) * ring_step + plane * plane_step + (k % 2) * 2 + other
        return remote(cot4.at[:, pl.ds(hi, HALF)], st.at[ring * 4 + z * 2 + c], s1.at[0], q1.at[ring], (rep, target))

    for d in range(8):
        if d:
            same_core(d).start()
        other_core(d).start()

    loads[4].wait()
    i0, i1 = selected_rows(plan_ref, frag_ref)
    msg[0:1, :] = lp[pl.ds(i0, 1), :].astype(BF)
    msg[1:2, :] = lp[pl.ds(i1, 1), :].astype(BF)
    swap = remote(msg, peer_msg, sx.at[0], qx.at[0], (1 - rep, f))
    swap.start()

    loads[1].wait()
    loads[2].wait()
    slope[...] = dot(x_v[...], wu[...], 1, 0)
    u = slope[...]
    t = jnp.tanh(0.7978845608 * (u + 0.044715 * u * u * u))
    hid[...] = (0.5 * u * (1.0 + t)).astype(BF)
    slope[...] = 0.5 * (1.0 + t) + 0.5 * u * (1.0 - t * t) * 0.7978845608 * (1.0 + 3.0 * 0.044715 * u * u)

    def block0(r, q):
        return cotg.at[r, q, :, pl.ds(0, HALF)]

    def block1(r, q):
        return cotg.at[q, r, :, pl.ds(HALF, HALF)]

    def ring_copy(block, e, d):
        b = block(ring, block_of(e))
        return remote(b, b, s3.at[0], q3.at[e, d - 1], on_ring((ring + d) % 4))

    def core_copy(block, e, d):
        b = block((ring + 4 - d) % 4, block_of(e))
        return remote(b, b, s4.at[0], q4.at[0], peer)

    def per_core(fn):
        @pl.when(c == 0)
        def _():
            fn(block0)

        @pl.when(c == 1)
        def _():
            fn(block1)

    def pieces(e):
        n = 4 if e else 3
        return remote(st.at[pl.ds(0, n)], st.at[pl.ds(0, n)], s1.at[0], q1.at[block_of(e)], peer)

    for e in NEAR:
        pieces(e).wait_recv()
        q = block_of(e)
        block = jnp.concatenate([st[4 * q + i].astype(F32) for i in range(4)], axis=0).astype(BF)

        def stage2(where):
            if where is block0:
                cotg[x, q, :, 0:HALF] = block
            else:
                cotg[q, y, :, HALF:] = block
            for d in (1, 3, 2):
                ring_copy(where, e, d).start()
            core_copy(where, e, 0).start()

        per_core(stage2)

    def across(n, cols):
        j = cols.start // cols.size
        return remote(sb.at[n, :, :, :, cols], rb.at[n, :, :, :, cols], s0.at[n, j], q0.at[n, j], peer)

    def first(n, chunks, product):
        for cols in chunks:
            sb[n, :, :, :, cols] = product(hi, cols).astype(BF).reshape(4, 4, 16, cols.size)
            across(n, cols).start()
        for cols in chunks:
            own[:, cols] = product(lo, cols)

    def first_done(n, cols):
        across(n, cols).wait_recv()
        total = own[:, cols].reshape(4, 4, 16, cols.size) + rb[n, :, :, :, cols].astype(F32)
        part[n, :, :, :, cols] = total.astype(BF)

    def second(n):
        for core in (0, 1):
            @pl.when(c == core)
            def _():
                for e in FAR:
                    q = block_of(e)
                    for d in (1, 3, 2):
                        r = (ring + d) % 4
                        src = part.at[n, r, q] if core == 0 else part.at[n, q, r]
                        remote(src, r1.at[n, d - 1, q], sr.at[n], qr.at[n, e], on_ring(r)).start()

    def third(n):
        slot = c * 8 + plane * 2 + z
        for e in FAR:
            q = block_of(e)
            got = r1.at[n, :, q]
            remote(got, got, sr.at[n], qr.at[n, e], peer).wait_recv()
            mine = jnp.where(c == 0, part[n, x, q].astype(F32), part[n, q, y].astype(F32))
            v = mine + r1[n, 0, q].astype(F32) + r1[n, 1, q].astype(F32) + r1[n, 2, q].astype(F32)
            for i in range(4):
                sp[n, 4 * q + i] = v[4 * i : 4 * i + 4].astype(BF)
            for i in range(0 if e else 1, 4):
                k = 4 * q + (z * 2 + c + i) % 4
                remote(sp.at[n, k], rp.at[n, slot], s2.at[n], q2.at[n], in_plane(k)).start()
        rp[n, slot] = sp[n, here]

    def third_all(n):
        return remote(sp.at[n, pl.ds(0, 15)], rp.at[n, pl.ds(0, 15)], s2.at[n], q2.at[n], peer)

    def third_done(n, out):
        third_all(n).wait_recv()
        for h in (0, 1):
            v = rp[n, 8 * h].astype(F32)
            for k in range(1, 8):
                v = v + rp[n, 8 * h + k].astype(F32)
            out[0, :, h * HALF : (h + 1) * HALF] = v.astype(BF)

    chunks = [pl.ds(j * HALF // PARTS, HALF // PARTS) for j in range(PARTS)]

    loads[3].wait()
    first(0, chunks, lambda at, cols: dot(hid[...], wd[:, pl.ds(at + cols.start, cols.size)], 1, 0))
    for cols in chunks:
        first_done(0, cols)

    loads[5].wait()
    loads[6].wait()
    swap.wait_recv()
    for e in range(0, 16384, 2048):
        cols = slice(e, e + 2048)
        mine, g, mom = lp[:, cols], gp[:, cols], om[:, cols]
        row = lax.broadcasted_iota(jnp.int32, mine.shape, 0)
        keep = (row == i0) | (row == i1)
        theirs = peer_msg[:, cols].astype(F32)
        far = jnp.where(row == i0, theirs[0:1, :], theirs[1:2, :])
        delta = g - (mine.astype(BF).astype(F32) + far) / 2
        momentum = 0.9 * mom + delta
        ng = jnp.where(keep, g - 0.7 * (delta + 0.9 * momentum), g)
        nm_ref[:, cols] = jnp.where(keep, momentum, mom)
        ng_ref[:, cols] = ng
        ml_ref[0, :, cols] = jnp.where(keep, 0.5 * mine + 0.5 * ng, mine)

    def stage3(where):
        for e in NEAR:
            for d in (1, 3, 2):
                ring_copy(where, e, d).wait_recv()
                core_copy(where, e, d).start()

    per_core(stage3)
    second(0)
    theirs = cotg.at[:, :, :, pl.ds(hi, HALF)]
    remote(theirs, theirs, s4.at[0], q4.at[0], peer).wait_recv()

    hg = dot(cotg[...].reshape(256, 4096), wd[...], 1, 1)
    pg[...] = (hg * slope[...]).astype(BF)
    first(1, chunks, lambda at, cols: dot(pg[...], wu[pl.ds(at + cols.start, cols.size), :], 1, 1))
    for cols in chunks:
        first_done(1, cols)
    second(1)
    third(0)

    dg_ref[0] = dot(hid[...], cotg[...].reshape(256, 4096), 0, 0).astype(BF)
    ug_ref[0] = dot(x_v[...], pg[...], 0, 0).astype(BF)
    third(1)
    third_done(0, bo_ref)
    third_done(1, ig_ref)

    swap.wait_send()
    remote(st.at[pl.ds(0, 15)], st.at[pl.ds(0, 15)], s1.at[0], q1.at[0], peer).wait_send()
    half = cotg.at[:, :, :, pl.ds(0, HALF)]
    most = cotg.at[pl.ds(0, 3), :, :, pl.ds(0, HALF)]
    remote(most, most, s3.at[0], q3.at[0, 0], peer).wait_send()
    remote(half, half, s4.at[0], q4.at[0], peer).wait_send()
    for n in (0, 1):
        for cols in chunks:
            across(n, cols).wait_send()
        remote(r1.at[n], r1.at[n], sr.at[n], qr.at[n, 0], peer).wait_send()
        third_all(n).wait_send()


def step_call(x, cot, wu, wd, lp, gp, om, plan, frag):
    hbm = pl.BlockSpec(memory_space=pl.ANY)
    smem = pl.BlockSpec(memory_space=pltpu.SMEM)
    vmem = pl.BlockSpec(memory_space=pltpu.VMEM)
    dma = pltpu.SemaphoreType.DMA
    return pl.pallas_call(
        step_kernel,
        out_shape=(
            pltpu.VMEM((1, 4, 4096), BF),
            pltpu.VMEM((1, 4, 4096), BF),
            pltpu.VMEM((1, 4096, 512), BF),
            pltpu.VMEM((1, 512, 4096), BF),
            pltpu.VMEM((16, 16384), F32),
            pltpu.VMEM((16, 16384), F32),
            pltpu.VMEM((1, 16, 16384), F32),
        ),
        in_specs=[hbm] * 7 + [smem, smem],
        out_specs=(vmem,) * 7,
        scratch_shapes=[
            pltpu.VMEM((256, 4096), BF),
            pltpu.VMEM((4096, 512), BF),
            pltpu.VMEM((512, 4096), BF),
            pltpu.VMEM((16, 16384), F32),
            pltpu.VMEM((16, 16384), F32),
            pltpu.VMEM((16, 16384), F32),
            pltpu.VMEM((4, 4096), BF),
            pltpu.VMEM((16, 4, HALF), BF),
            pltpu.VMEM((4, 4, 16, 4096), BF),
            pltpu.VMEM((256, 512), F32),
            pltpu.VMEM((256, 512), BF),
            pltpu.VMEM((256, 512), BF),
            pltpu.VMEM((2, 16384), BF),
            pltpu.VMEM((2, 16384), BF),
            pltpu.VMEM((256, HALF), F32),
            pltpu.VMEM((2, 4, 4, 16, HALF), BF),
            pltpu.VMEM((2, 4, 4, 16, HALF), BF),
            pltpu.VMEM((2, 4, 4, 16, HALF), BF),
            pltpu.VMEM((2, 3, 4, 16, HALF), BF),
            pltpu.VMEM((2, 16, 4, HALF), BF),
            pltpu.VMEM((2, 16, 4, HALF), BF),
            dma((7,)),
            dma((1,)), dma((4,)),
            dma((1,)), dma((4, 3)),
            dma((1,)), dma((1,)),
            dma((2, PARTS)), dma((2, PARTS)),
            dma((2,)), dma((2, 4)),
            dma((2,)), dma((2,)),
            dma((1,)), dma((1,)),
        ],
        compiler_params=pltpu.CompilerParams(collective_id=1, has_side_effects=True, vmem_limit_bytes=46 << 20),
        cost_estimate=pl.CostEstimate(flops=6 * 2 * 256 * 4096 * 512, bytes_accessed=14 << 20, transcendentals=1 << 17),
    )(x, cot, wu, wd, lp, gp, om, plan, frag)


def write_kernel(*refs):
    n = len(refs) // 2
    copies = [pltpu.make_async_copy(refs[i], refs[n + i], refs[2 * n].at[i]) for i in range(n)]
    for copy in copies:
        copy.start()
    for copy in copies:
        copy.wait()


def write_call(*arrays):
    n = len(arrays)
    return pl.pallas_call(
        write_kernel,
        out_shape=tuple(jax.ShapeDtypeStruct(a.shape, a.dtype) for a in arrays),
        in_specs=[pl.BlockSpec(memory_space=pltpu.VMEM)] * n,
        out_specs=tuple(pl.BlockSpec(memory_space=pl.ANY) for _ in arrays),
        scratch_shapes=[pltpu.SemaphoreType.DMA((n,))],
        compiler_params=pltpu.CompilerParams(has_side_effects=True, vmem_limit_bytes=16 << 20),
        cost_estimate=pl.CostEstimate(flops=0, bytes_accessed=12 << 20, transcendentals=0),
    )(*arrays)


def on_device(inputs, cotangent, up_weight, down_weight, local_params, global_params, outer_momentum, plan, fragment_id):
    return write_call(
        *step_call(
            inputs, cotangent, up_weight, down_weight, local_params, global_params, outer_momentum, plan, fragment_id
        )
    )


def solution(mesh):
    placed = (
        P("replica", None, None),
        P("replica", "fsdp", None),
        P("replica", None, "fsdp"),
        P("replica", "fsdp", None),
        P("replica", None, "fsdp"),
        P(None, "fsdp"),
        P(None, "fsdp"),
        P(),
        P(),
    )
    return jax.shard_map(
        on_device,
        mesh=mesh,
        in_specs=placed,
        out_specs=(
            P("replica", "fsdp", None),
            P("replica", "fsdp", None),
            P("replica", None, "fsdp"),
            P("replica", "fsdp", None),
            P(None, "fsdp"),
            P(None, "fsdp"),
            P("replica", None, "fsdp"),
        ),
        check_vma=False,
    )
```

```python
import jax
import jax.numpy as jnp
from jax import lax
from jax.experimental import pallas as pl
from jax.experimental.pallas import tpu as pltpu
from jax.sharding import PartitionSpec as P

BF = jnp.bfloat16
F32 = jnp.float32
MESH = pl.DeviceIdType.MESH
HALF = 2048
NEAR = (0, 1, 3, 2)
FAR = (2, 1, 3, 0)


def dot(a, b, ca, cb):
    return lax.dot_general(a, b, (((ca,), (cb,)), ((), ())), preferred_element_type=F32)


def selected_rows(plan_ref, frag_ref):
    first, last = jnp.int32(15), jnp.int32(0)
    for layer in range(16):
        hit = plan_ref[layer] == frag_ref[0]
        first = jnp.minimum(first, jnp.where(hit, layer, 15))
        last = jnp.maximum(last, jnp.where(hit, layer, 0))
    return first, last


def step_kernel(
    x_hbm, cot_hbm, wu_hbm, wd_hbm, lp_hbm, gp_hbm, om_hbm, plan_hbm, frag_hbm,
    bo_ref, ig_ref, ug_ref, dg_ref, ng_ref, nm_ref, ml_ref,
    plan_ref, frag_ref, x_v, wu, wd, lp, gp, om, cot4, st, cotg, slope, hg, hid, pg, msg, peer_msg,
    own, sb, rb, part, r1, sp, rp,
    lsem, s1, q1, s3, q3, s4, q4, s0, q0, sr, qr, s2, q2, sx, qx,
):
    rep = lax.axis_index("replica")
    f = lax.axis_index("fsdp")
    x, y, z, c = f // 16, (f // 4) % 4, (f // 2) % 2, f % 2
    other = 1 - c
    lo = pl.multiple_of(c * HALF, HALF)
    hi = pl.multiple_of(other * HALF, HALF)
    ring = jnp.where(c == 0, x, y)
    plane = jnp.where(c == 0, y, x)

    ring_step = jnp.where(c == 0, 16, 4)
    plane_step = jnp.where(c == 0, 4, 16)
    here = plane * 4 + z * 2 + c
    peer = (rep, f + other - c)

    def on_ring(r):
        return (rep, f + (r - ring) * ring_step)

    def in_plane(k):
        return (rep, ring * ring_step + (k // 4) * plane_step + k % 4)

    def block_of(e):
        return (plane + e) % 4

    def rotate(k, fn):
        lax.fori_loop(1, 16, lambda d, _: (fn((k + d) % 16), 0)[1], 0)

    def remote(src, dst, ssem, rsem, device):
        return pltpu.make_async_remote_copy(
            src_ref=src, dst_ref=dst, send_sem=ssem, recv_sem=rsem, device_id=device, device_id_type=MESH
        )

    barrier = pltpu.get_barrier_semaphore()

    rotate(here, lambda k: pl.semaphore_signal(barrier, inc=1, device_id=in_plane(k), device_id_type=MESH))
    for d in (1, 2, 3):
        pl.semaphore_signal(barrier, inc=1, device_id=on_ring((ring + d) % 4), device_id_type=MESH)
    pl.semaphore_signal(barrier, inc=1, device_id=(1 - rep, f), device_id_type=MESH)

    loads = [
        pltpu.make_async_copy(cot_hbm.at[0], cot4, lsem.at[0]),
        pltpu.make_async_copy(x_hbm.at[0], x_v, lsem.at[1]),
        pltpu.make_async_copy(wu_hbm.at[0], wu, lsem.at[2]),
        pltpu.make_async_copy(wd_hbm.at[0], wd, lsem.at[3]),
        pltpu.make_async_copy(lp_hbm.at[0], lp, lsem.at[4]),
        pltpu.make_async_copy(gp_hbm, gp, lsem.at[5]),
        pltpu.make_async_copy(om_hbm, om, lsem.at[6]),
        pltpu.make_async_copy(plan_hbm, plan_ref, lsem.at[7]),
        pltpu.make_async_copy(frag_hbm, frag_ref, lsem.at[8]),
    ]
    for k in (0, 7, 8, 1, 2, 4, 3, 5, 6):
        loads[k].start()
    pl.semaphore_wait(barrier, 19)

    loads[0].wait()
    st[here] = cot4[:, pl.ds(lo, HALF)]

    def same_core(d):
        k = (plane * 2 + z + d) % 8
        target = ring * ring_step + (k // 2) * plane_step + (k % 2) * 2 + c
        return remote(cot4.at[:, pl.ds(lo, HALF)], st.at[here], s1.at[0], q1.at[plane], (rep, target))

    def other_core(d):
        k = (ring * 2 + z + d) % 8
        target = (k // 2) * ring_step + plane * plane_step + (k % 2) * 2 + other
        return remote(cot4.at[:, pl.ds(hi, HALF)], st.at[ring * 4 + z * 2 + c], s1.at[0], q1.at[ring], (rep, target))

    for d in range(8):
        if d:
            same_core(d).start()
        other_core(d).start()

    loads[4].wait()
    loads[7].wait()
    loads[8].wait()
    i0, i1 = selected_rows(plan_ref, frag_ref)
    msg[0:1, :] = lp[pl.ds(i0, 1), :].astype(BF)
    msg[1:2, :] = lp[pl.ds(i1, 1), :].astype(BF)
    swap = remote(msg, peer_msg, sx.at[0], qx.at[0], (1 - rep, f))
    swap.start()

    loads[1].wait()
    loads[2].wait()
    slope[...] = dot(x_v[...], wu[...], 1, 0)
    u = slope[...]
    t = jnp.tanh(0.7978845608 * (u + 0.044715 * u * u * u))
    hid[...] = (0.5 * u * (1.0 + t)).astype(BF)
    slope[...] = 0.5 * (1.0 + t) + 0.5 * u * (1.0 - t * t) * 0.7978845608 * (1.0 + 3.0 * 0.044715 * u * u)

    def block0(r, q):
        return cotg.at[r, q, :, pl.ds(0, HALF)]

    def block1(r, q):
        return cotg.at[q, r, :, pl.ds(HALF, HALF)]

    def ring_copy(block, e, d):
        b = block(ring, block_of(e))
        return remote(b, b, s3.at[0], q3.at[e, d - 1], on_ring((ring + d) % 4))

    def core_copy(block, e, d):
        b = block((ring + 4 - d) % 4, block_of(e))
        return remote(b, b, s4.at[0], q4.at[0], peer)

    def per_core(fn):
        @pl.when(c == 0)
        def _():
            fn(block0)

        @pl.when(c == 1)
        def _():
            fn(block1)

    def pieces(e):
        n = 4 if e else 3
        return remote(st.at[pl.ds(0, n)], st.at[pl.ds(0, n)], s1.at[0], q1.at[block_of(e)], peer)

    for e in NEAR:
        pieces(e).wait_recv()
        q = block_of(e)
        block = jnp.concatenate([st[4 * q + i].astype(F32) for i in range(4)], axis=0).astype(BF)

        def stage2(where):
            if where is block0:
                cotg[x, q, :, 0:HALF] = block
            else:
                cotg[q, y, :, HALF:] = block
            for d in (1, 3, 2):
                ring_copy(where, e, d).start()
            core_copy(where, e, 0).start()

        per_core(stage2)

    def first(n, product):
        sb[n] = product(hi).astype(BF).reshape(4, 4, 16, HALF)
        for core in (0, 1):
            @pl.when(c == core)
            def _():
                for e in FAR:
                    q = (ring + e) % 4
                    src, dst = (sb.at[n, q], rb.at[n, q]) if core == 0 else (sb.at[n, :, q], rb.at[n, :, q])
                    remote(src, dst, s0.at[n], q0.at[n, e], peer).start()
        own[...] = product(lo).reshape(4, 4, 16, HALF)

    def combine(n, core, e):
        q = block_of(e)
        remote(rb.at[n, 0], rb.at[n, 0], s0.at[n], q0.at[n, e], peer).wait_recv()
        if core == 0:
            part[n, :, q] = (own[:, q] + rb[n, :, q].astype(F32)).astype(BF)
        else:
            part[n, q] = (own[q] + rb[n, q].astype(F32)).astype(BF)

    def ring_send(n, core, e):
        q = block_of(e)
        for d in (1, 3, 2):
            r = (ring + d) % 4
            src = part.at[n, r, q] if core == 0 else part.at[n, q, r]
            remote(src, r1.at[n, d - 1, q], sr.at[n], qr.at[n, e], on_ring(r)).start()

    def blocks(*acts):
        for core in (0, 1):
            @pl.when(c == core)
            def _():
                for e in FAR:
                    for act in acts:
                        act(core, e)

    def third(n):
        slot = c * 8 + plane * 2 + z
        for e in FAR:
            q = block_of(e)
            got = r1.at[n, :, q]
            remote(got, got, sr.at[n], qr.at[n, e], peer).wait_recv()
            mine = jnp.where(c == 0, part[n, x, q].astype(F32), part[n, q, y].astype(F32))
            v = mine + r1[n, 0, q].astype(F32) + r1[n, 1, q].astype(F32) + r1[n, 2, q].astype(F32)
            for i in range(4):
                sp[n, 4 * q + i] = v[4 * i : 4 * i + 4].astype(BF)
            for i in range(0 if e else 1, 4):
                k = 4 * q + (z * 2 + c + i) % 4
                remote(sp.at[n, k], rp.at[n, slot], s2.at[n], q2.at[n], in_plane(k)).start()
        rp[n, slot] = sp[n, here]

    def third_all(n):
        return remote(sp.at[n, pl.ds(0, 15)], rp.at[n, pl.ds(0, 15)], s2.at[n], q2.at[n], peer)

    def third_done(n, out):
        third_all(n).wait_recv()
        for h in (0, 1):
            v = rp[n, 8 * h].astype(F32)
            for k in range(1, 8):
                v = v + rp[n, 8 * h + k].astype(F32)
            out[0, :, h * HALF : (h + 1) * HALF] = v.astype(BF)

    loads[3].wait()
    first(0, lambda at: dot(hid[...], wd[:, pl.ds(at, HALF)], 1, 0))
    blocks(lambda core, e: combine(0, core, e))

    loads[5].wait()
    loads[6].wait()
    swap.wait_recv()
    for e in range(0, 16384, 2048):
        cols = slice(e, e + 2048)
        mine, g, mom = lp[:, cols], gp[:, cols], om[:, cols]
        row = lax.broadcasted_iota(jnp.int32, mine.shape, 0)
        keep = (row == i0) | (row == i1)
        theirs = peer_msg[:, cols].astype(F32)
        far = jnp.where(row == i0, theirs[0:1, :], theirs[1:2, :])
        delta = g - (mine.astype(BF).astype(F32) + far) / 2
        momentum = 0.9 * mom + delta
        ng = jnp.where(keep, g - 0.7 * (delta + 0.9 * momentum), g)
        nm_ref[:, cols] = jnp.where(keep, momentum, mom)
        ng_ref[:, cols] = ng
        ml_ref[0, :, cols] = jnp.where(keep, 0.5 * mine + 0.5 * ng, mine)

    def stage3(where):
        for i, e in enumerate(NEAR):
            if i == 3:
                most = cotg.at[pl.ds(0, 3), :, :, pl.ds(0, HALF)]
                remote(most, most, s3.at[0], q3.at[0, 0], peer).wait_send()
                for b in FAR:
                    ring_send(0, 0 if where is block0 else 1, b)
            for d in (1, 3, 2):
                ring_copy(where, e, d).wait_recv()
                core_copy(where, e, d).start()

    per_core(stage3)

    def half_grad(at):
        return dot(cotg[:, :, :, pl.ds(at, HALF)].reshape(256, HALF), wd[:, pl.ds(at, HALF)], 1, 1)

    hg[...] = half_grad(lo)
    theirs = cotg.at[:, :, :, pl.ds(hi, HALF)]
    remote(theirs, theirs, s4.at[0], q4.at[0], peer).wait_recv()

    pg[...] = ((hg[...] + half_grad(hi)) * slope[...]).astype(BF)
    first(1, lambda at: dot(pg[...], wu[pl.ds(at, HALF), :], 1, 1))
    blocks(lambda core, e: combine(1, core, e), lambda core, e: ring_send(1, core, e))

    dg_ref[0] = dot(hid[...], cotg[...].reshape(256, 4096), 0, 0).astype(BF)
    ug_ref[0] = dot(x_v[...], pg[...], 0, 0).astype(BF)
    third(0)
    third(1)
    third_done(0, bo_ref)
    third_done(1, ig_ref)

    swap.wait_send()
    remote(st.at[pl.ds(0, 15)], st.at[pl.ds(0, 15)], s1.at[0], q1.at[0], peer).wait_send()
    half = cotg.at[:, :, :, pl.ds(0, HALF)]
    remote(half, half, s4.at[0], q4.at[0], peer).wait_send()
    for n in (0, 1):
        remote(sb.at[n], rb.at[n], s0.at[n], q0.at[n, 0], peer).wait_send()
        remote(r1.at[n], r1.at[n], sr.at[n], qr.at[n, 0], peer).wait_send()
        third_all(n).wait_send()


def step_call(x, cot, wu, wd, lp, gp, om, plan, frag):
    hbm = pl.BlockSpec(memory_space=pl.ANY)
    smem = pl.BlockSpec(memory_space=pltpu.SMEM)
    vmem = pl.BlockSpec(memory_space=pltpu.VMEM)
    dma = pltpu.SemaphoreType.DMA
    return pl.pallas_call(
        step_kernel,
        out_shape=(
            pltpu.VMEM((1, 4, 4096), BF),
            pltpu.VMEM((1, 4, 4096), BF),
            pltpu.VMEM((1, 4096, 512), BF),
            pltpu.VMEM((1, 512, 4096), BF),
            pltpu.VMEM((16, 16384), F32),
            pltpu.VMEM((16, 16384), F32),
            pltpu.VMEM((1, 16, 16384), F32),
        ),
        in_specs=[hbm] * 9,
        out_specs=(vmem,) * 7,
        scratch_shapes=[
            pltpu.SMEM((16,), jnp.int32),
            pltpu.SMEM((1,), jnp.int32),
            pltpu.VMEM((256, 4096), BF),
            pltpu.VMEM((4096, 512), BF),
            pltpu.VMEM((512, 4096), BF),
            pltpu.VMEM((16, 16384), F32),
            pltpu.VMEM((16, 16384), F32),
            pltpu.VMEM((16, 16384), F32),
            pltpu.VMEM((4, 4096), BF),
            pltpu.VMEM((16, 4, HALF), BF),
            pltpu.VMEM((4, 4, 16, 4096), BF),
            pltpu.VMEM((256, 512), F32),
            pltpu.VMEM((256, 512), F32),
            pltpu.VMEM((256, 512), BF),
            pltpu.VMEM((256, 512), BF),
            pltpu.VMEM((2, 16384), BF),
            pltpu.VMEM((2, 16384), BF),
            pltpu.VMEM((4, 4, 16, HALF), F32),
            pltpu.VMEM((2, 4, 4, 16, HALF), BF),
            pltpu.VMEM((2, 4, 4, 16, HALF), BF),
            pltpu.VMEM((2, 4, 4, 16, HALF), BF),
            pltpu.VMEM((2, 3, 4, 16, HALF), BF),
            pltpu.VMEM((2, 16, 4, HALF), BF),
            pltpu.VMEM((2, 16, 4, HALF), BF),
            dma((9,)),
            dma((1,)), dma((4,)),
            dma((1,)), dma((4, 3)),
            dma((1,)), dma((1,)),
            dma((2,)), dma((2, 4)),
            dma((2,)), dma((2, 4)),
            dma((2,)), dma((2,)),
            dma((1,)), dma((1,)),
        ],
        compiler_params=pltpu.CompilerParams(collective_id=1, has_side_effects=True, vmem_limit_bytes=46 << 20),
        cost_estimate=pl.CostEstimate(flops=6 * 2 * 256 * 4096 * 512, bytes_accessed=14 << 20, transcendentals=1 << 17),
    )(x, cot, wu, wd, lp, gp, om, plan, frag)


def write_kernel(*refs):
    n = len(refs) // 2
    copies = [pltpu.make_async_copy(refs[i], refs[n + i], refs[2 * n].at[i]) for i in range(n)]
    for copy in copies:
        copy.start()
    for copy in copies:
        copy.wait()


def write_call(*arrays):
    n = len(arrays)
    return pl.pallas_call(
        write_kernel,
        out_shape=tuple(jax.ShapeDtypeStruct(a.shape, a.dtype) for a in arrays),
        in_specs=[pl.BlockSpec(memory_space=pltpu.VMEM)] * n,
        out_specs=tuple(pl.BlockSpec(memory_space=pl.ANY) for _ in arrays),
        scratch_shapes=[pltpu.SemaphoreType.DMA((n,))],
        compiler_params=pltpu.CompilerParams(has_side_effects=True, vmem_limit_bytes=16 << 20),
        cost_estimate=pl.CostEstimate(flops=0, bytes_accessed=12 << 20, transcendentals=0),
    )(*arrays)


def on_device(inputs, cotangent, up_weight, down_weight, local_params, global_params, outer_momentum, plan, fragment_id):
    return write_call(
        *step_call(
            inputs, cotangent, up_weight, down_weight, local_params, global_params, outer_momentum, plan, fragment_id
        )
    )


def solution(mesh):
    placed = (
        P("replica", None, None),
        P("replica", "fsdp", None),
        P("replica", None, "fsdp"),
        P("replica", "fsdp", None),
        P("replica", None, "fsdp"),
        P(None, "fsdp"),
        P(None, "fsdp"),
        P(),
        P(),
    )
    return jax.shard_map(
        on_device,
        mesh=mesh,
        in_specs=placed,
        out_specs=(
            P("replica", "fsdp", None),
            P("replica", "fsdp", None),
            P("replica", None, "fsdp"),
            P("replica", "fsdp", None),
            P(None, "fsdp"),
            P(None, "fsdp"),
            P("replica", None, "fsdp"),
        ),
        check_vma=False,
    )
```

```python
import jax
import jax.numpy as jnp
from jax import lax
from jax.experimental import pallas as pl
from jax.experimental.pallas import tpu as pltpu
from jax.sharding import PartitionSpec as P

BF = jnp.bfloat16
F32 = jnp.float32
MESH = pl.DeviceIdType.MESH
HALF = 2048
NEAR = (0, 1, 3, 2)
FAR = (2, 1, 3, 0)


def dot(a, b, ca, cb):
    return lax.dot_general(a, b, (((ca,), (cb,)), ((), ())), preferred_element_type=F32)


def selected_rows(plan_ref, frag_ref):
    first, last = jnp.int32(15), jnp.int32(0)
    for layer in range(16):
        hit = plan_ref[layer] == frag_ref[0]
        first = jnp.minimum(first, jnp.where(hit, layer, 15))
        last = jnp.maximum(last, jnp.where(hit, layer, 0))
    return first, last


def step_kernel(
    x_hbm, cot_hbm, wu_hbm, wd_hbm, lp_hbm, gp_hbm, om_hbm, plan_hbm, frag_hbm,
    bo_ref, ig_ref, ug_ref, dg_ref, ng_ref, nm_ref, ml_ref,
    plan_ref, frag_ref, x_v, wu, wd, lp, gp, om, cot4, st, cotg, slope, hg, hid, pg, msg, peer_msg,
    own, sb, rb, part, r1, sp, rp,
    lsem, s1, q1, s3, q3, s4, q4, s0, q0, sr, qr, s2, q2, sx, qx,
):
    rep = lax.axis_index("replica")
    f = lax.axis_index("fsdp")
    x, y, z, c = f // 16, (f // 4) % 4, (f // 2) % 2, f % 2
    other = 1 - c
    lo = pl.multiple_of(c * HALF, HALF)
    hi = pl.multiple_of(other * HALF, HALF)
    ring = jnp.where(c == 0, x, y)
    plane = jnp.where(c == 0, y, x)

    ring_step = jnp.where(c == 0, 16, 4)
    plane_step = jnp.where(c == 0, 4, 16)
    here = plane * 4 + z * 2 + c
    peer = (rep, f + other - c)

    def on_ring(r):
        return (rep, f + (r - ring) * ring_step)

    def in_plane(k):
        return (rep, ring * ring_step + (k // 4) * plane_step + k % 4)

    def block_of(e):
        return (plane + e) % 4

    def rotate(k, fn):
        lax.fori_loop(1, 16, lambda d, _: (fn((k + d) % 16), 0)[1], 0)

    def remote(src, dst, ssem, rsem, device):
        return pltpu.make_async_remote_copy(
            src_ref=src, dst_ref=dst, send_sem=ssem, recv_sem=rsem, device_id=device, device_id_type=MESH
        )

    barrier = pltpu.get_barrier_semaphore()

    rotate(here, lambda k: pl.semaphore_signal(barrier, inc=1, device_id=in_plane(k), device_id_type=MESH))
    for d in (1, 2, 3):
        pl.semaphore_signal(barrier, inc=1, device_id=on_ring((ring + d) % 4), device_id_type=MESH)
    pl.semaphore_signal(barrier, inc=1, device_id=(1 - rep, f), device_id_type=MESH)

    loads = [
        pltpu.make_async_copy(cot_hbm.at[0], cot4, lsem.at[0]),
        pltpu.make_async_copy(x_hbm.at[0], x_v, lsem.at[1]),
        pltpu.make_async_copy(wu_hbm.at[0], wu, lsem.at[2]),
        pltpu.make_async_copy(wd_hbm.at[0], wd, lsem.at[3]),
        pltpu.make_async_copy(lp_hbm.at[0], lp, lsem.at[4]),
        pltpu.make_async_copy(gp_hbm, gp, lsem.at[5]),
        pltpu.make_async_copy(om_hbm, om, lsem.at[6]),
        pltpu.make_async_copy(plan_hbm, plan_ref, lsem.at[7]),
        pltpu.make_async_copy(frag_hbm, frag_ref, lsem.at[8]),
    ]
    for k in (0, 1, 2, 3, 7, 8, 4, 5, 6):
        loads[k].start()
    pl.semaphore_wait(barrier, 19)

    loads[0].wait()
    st[here] = cot4[:, pl.ds(lo, HALF)]

    def same_core(d):
        target = ring * ring_step + block_of(NEAR[d // 2]) * plane_step + (z + d) % 2 * 2 + c
        return remote(cot4.at[:, pl.ds(lo, HALF)], st.at[here], s1.at[0], q1.at[plane], (rep, target))

    def other_core(d):
        target = (ring + NEAR[d // 2]) % 4 * ring_step + plane * plane_step + (z + d) % 2 * 2 + other
        return remote(cot4.at[:, pl.ds(hi, HALF)], st.at[ring * 4 + z * 2 + c], s1.at[0], q1.at[ring], (rep, target))

    for d in range(8):
        if d:
            same_core(d).start()
        other_core(d).start()

    loads[1].wait()
    loads[2].wait()
    slope[...] = dot(x_v[...], wu[...], 1, 0)
    u = slope[...]
    t = jnp.tanh(0.7978845608 * (u + 0.044715 * u * u * u))
    hid[...] = (0.5 * u * (1.0 + t)).astype(BF)
    slope[...] = 0.5 * (1.0 + t) + 0.5 * u * (1.0 - t * t) * 0.7978845608 * (1.0 + 3.0 * 0.044715 * u * u)

    def block0(r, q):
        return cotg.at[r, q, :, pl.ds(0, HALF)]

    def block1(r, q):
        return cotg.at[q, r, :, pl.ds(HALF, HALF)]

    def ring_copy(block, e, d):
        b = block(ring, block_of(e))
        return remote(b, b, s3.at[0], q3.at[e, d - 1], on_ring((ring + d) % 4))

    def core_copy(block, e, d):
        b = block((ring + 4 - d) % 4, block_of(e))
        return remote(b, b, s4.at[0], q4.at[0], peer)

    def per_core(fn):
        @pl.when(c == 0)
        def _():
            fn(block0)

        @pl.when(c == 1)
        def _():
            fn(block1)

    def pieces(e):
        n = 4 if e else 3
        return remote(st.at[pl.ds(0, n)], st.at[pl.ds(0, n)], s1.at[0], q1.at[block_of(e)], peer)

    for e in NEAR:
        pieces(e).wait_recv()
        q = block_of(e)
        block = jnp.concatenate([st[4 * q + i].astype(F32) for i in range(4)], axis=0).astype(BF)

        def stage2(where):
            if where is block0:
                cotg[x, q, :, 0:HALF] = block
            else:
                cotg[q, y, :, HALF:] = block
            for d in (2, 1, 3):
                ring_copy(where, e, d).start()
            core_copy(where, e, 0).start()

        per_core(stage2)

    loads[4].wait()
    loads[7].wait()
    loads[8].wait()
    i0, i1 = selected_rows(plan_ref, frag_ref)
    msg[0:1, :] = lp[pl.ds(i0, 1), :].astype(BF)
    msg[1:2, :] = lp[pl.ds(i1, 1), :].astype(BF)
    swap = remote(msg, peer_msg, sx.at[0], qx.at[0], (1 - rep, f))
    swap.start()

    def first(n, product):
        sb[n] = product(hi).astype(BF).reshape(4, 4, 16, HALF)
        for core in (0, 1):
            @pl.when(c == core)
            def _():
                for e in FAR:
                    q = (ring + e) % 4
                    src, dst = (sb.at[n, q], rb.at[n, q]) if core == 0 else (sb.at[n, :, q], rb.at[n, :, q])
                    remote(src, dst, s0.at[n], q0.at[n, e], peer).start()
        own[...] = product(lo).reshape(4, 4, 16, HALF)

    def combine(n, core, e):
        q = block_of(e)
        remote(rb.at[n, 0], rb.at[n, 0], s0.at[n], q0.at[n, e], peer).wait_recv()
        if core == 0:
            part[n, :, q] = (own[:, q] + rb[n, :, q].astype(F32)).astype(BF)
        else:
            part[n, q] = (own[q] + rb[n, q].astype(F32)).astype(BF)

    def ring_send(n, core, e):
        q = block_of(e)
        for d in (2, 1, 3):
            r = (ring + d) % 4
            src = part.at[n, r, q] if core == 0 else part.at[n, q, r]
            remote(src, r1.at[n, d - 1, q], sr.at[n], qr.at[n, e], on_ring(r)).start()

    def blocks(*acts):
        for core in (0, 1):
            @pl.when(c == core)
            def _():
                for e in FAR:
                    for act in acts:
                        act(core, e)

    def third(n):
        slot = c * 8 + plane * 2 + z
        for e in FAR:
            q = block_of(e)
            got = r1.at[n, :, q]
            remote(got, got, sr.at[n], qr.at[n, e], peer).wait_recv()
            mine = jnp.where(c == 0, part[n, x, q].astype(F32), part[n, q, y].astype(F32))
            v = mine + r1[n, 0, q].astype(F32) + r1[n, 1, q].astype(F32) + r1[n, 2, q].astype(F32)
            for i in range(4):
                sp[n, 4 * q + i] = v[4 * i : 4 * i + 4].astype(BF)
            for i in (2, 3, 0, 1) if e else (2, 3, 1):
                k = 4 * q + (z * 2 + c + i) % 4
                remote(sp.at[n, k], rp.at[n, slot], s2.at[n], q2.at[n], in_plane(k)).start()
        rp[n, slot] = sp[n, here]

    def third_all(n):
        return remote(sp.at[n, pl.ds(0, 15)], rp.at[n, pl.ds(0, 15)], s2.at[n], q2.at[n], peer)

    def third_done(n, out):
        third_all(n).wait_recv()
        for h in (0, 1):
            v = rp[n, 8 * h].astype(F32)
            for k in range(1, 8):
                v = v + rp[n, 8 * h + k].astype(F32)
            out[0, :, h * HALF : (h + 1) * HALF] = v.astype(BF)

    loads[3].wait()
    first(0, lambda at: dot(hid[...], wd[:, pl.ds(at, HALF)], 1, 0))
    blocks(lambda core, e: combine(0, core, e))

    def stage3(where):
        for i, e in enumerate(NEAR):
            if i == 3:
                most = cotg.at[pl.ds(0, 3), :, :, pl.ds(0, HALF)]
                remote(most, most, s3.at[0], q3.at[0, 0], peer).wait_send()
                for b in FAR:
                    ring_send(0, 0 if where is block0 else 1, b)
            for d in (2, 1, 3):
                ring_copy(where, e, d).wait_recv()
                core_copy(where, e, d).start()

    per_core(stage3)

    def half_grad(at):
        return dot(cotg[:, :, :, pl.ds(at, HALF)].reshape(256, HALF), wd[:, pl.ds(at, HALF)], 1, 1)

    hg[...] = half_grad(lo)
    theirs = cotg.at[:, :, :, pl.ds(hi, HALF)]
    remote(theirs, theirs, s4.at[0], q4.at[0], peer).wait_recv()

    pg[...] = ((hg[...] + half_grad(hi)) * slope[...]).astype(BF)
    first(1, lambda at: dot(pg[...], wu[pl.ds(at, HALF), :], 1, 1))
    blocks(lambda core, e: combine(1, core, e), lambda core, e: ring_send(1, core, e))

    dg_ref[0] = dot(hid[...], cotg[...].reshape(256, 4096), 0, 0).astype(BF)
    ug_ref[0] = dot(x_v[...], pg[...], 0, 0).astype(BF)
    third(0)
    third(1)

    loads[5].wait()
    loads[6].wait()
    swap.wait_recv()
    for e in range(0, 16384, 2048):
        cols = slice(e, e + 2048)
        mine, g, mom = lp[:, cols], gp[:, cols], om[:, cols]
        row = lax.broadcasted_iota(jnp.int32, mine.shape, 0)
        keep = (row == i0) | (row == i1)
        theirs = peer_msg[:, cols].astype(F32)
        far = jnp.where(row == i0, theirs[0:1, :], theirs[1:2, :])
        delta = g - (mine.astype(BF).astype(F32) + far) / 2
        momentum = 0.9 * mom + delta
        ng = jnp.where(keep, g - 0.7 * (delta + 0.9 * momentum), g)
        nm_ref[:, cols] = jnp.where(keep, momentum, mom)
        ng_ref[:, cols] = ng
        ml_ref[0, :, cols] = jnp.where(keep, 0.5 * mine + 0.5 * ng, mine)

    third_done(0, bo_ref)
    third_done(1, ig_ref)

    swap.wait_send()
    remote(st.at[pl.ds(0, 15)], st.at[pl.ds(0, 15)], s1.at[0], q1.at[0], peer).wait_send()
    half = cotg.at[:, :, :, pl.ds(0, HALF)]
    remote(half, half, s4.at[0], q4.at[0], peer).wait_send()
    for n in (0, 1):
        remote(sb.at[n], rb.at[n], s0.at[n], q0.at[n, 0], peer).wait_send()
        remote(r1.at[n], r1.at[n], sr.at[n], qr.at[n, 0], peer).wait_send()
        third_all(n).wait_send()


def step_call(x, cot, wu, wd, lp, gp, om, plan, frag):
    hbm = pl.BlockSpec(memory_space=pl.ANY)
    smem = pl.BlockSpec(memory_space=pltpu.SMEM)
    vmem = pl.BlockSpec(memory_space=pltpu.VMEM)
    dma = pltpu.SemaphoreType.DMA
    return pl.pallas_call(
        step_kernel,
        out_shape=(
            pltpu.VMEM((1, 4, 4096), BF),
            pltpu.VMEM((1, 4, 4096), BF),
            pltpu.VMEM((1, 4096, 512), BF),
            pltpu.VMEM((1, 512, 4096), BF),
            pltpu.VMEM((16, 16384), F32),
            pltpu.VMEM((16, 16384), F32),
            pltpu.VMEM((1, 16, 16384), F32),
        ),
        in_specs=[hbm] * 9,
        out_specs=(vmem,) * 7,
        scratch_shapes=[
            pltpu.SMEM((16,), jnp.int32),
            pltpu.SMEM((1,), jnp.int32),
            pltpu.VMEM((256, 4096), BF),
            pltpu.VMEM((4096, 512), BF),
            pltpu.VMEM((512, 4096), BF),
            pltpu.VMEM((16, 16384), F32),
            pltpu.VMEM((16, 16384), F32),
            pltpu.VMEM((16, 16384), F32),
            pltpu.VMEM((4, 4096), BF),
            pltpu.VMEM((16, 4, HALF), BF),
            pltpu.VMEM((4, 4, 16, 4096), BF),
            pltpu.VMEM((256, 512), F32),
            pltpu.VMEM((256, 512), F32),
            pltpu.VMEM((256, 512), BF),
            pltpu.VMEM((256, 512), BF),
            pltpu.VMEM((2, 16384), BF),
            pltpu.VMEM((2, 16384), BF),
            pltpu.VMEM((4, 4, 16, HALF), F32),
            pltpu.VMEM((2, 4, 4, 16, HALF), BF),
            pltpu.VMEM((2, 4, 4, 16, HALF), BF),
            pltpu.VMEM((2, 4, 4, 16, HALF), BF),
            pltpu.VMEM((2, 3, 4, 16, HALF), BF),
            pltpu.VMEM((2, 16, 4, HALF), BF),
            pltpu.VMEM((2, 16, 4, HALF), BF),
            dma((9,)),
            dma((1,)), dma((4,)),
            dma((1,)), dma((4, 3)),
            dma((1,)), dma((1,)),
            dma((2,)), dma((2, 4)),
            dma((2,)), dma((2, 4)),
            dma((2,)), dma((2,)),
            dma((1,)), dma((1,)),
        ],
        compiler_params=pltpu.CompilerParams(collective_id=1, has_side_effects=True, vmem_limit_bytes=46 << 20),
        cost_estimate=pl.CostEstimate(flops=6 * 2 * 256 * 4096 * 512, bytes_accessed=14 << 20, transcendentals=1 << 17),
    )(x, cot, wu, wd, lp, gp, om, plan, frag)


def write_kernel(*refs):
    n = len(refs) // 2
    copies = [pltpu.make_async_copy(refs[i], refs[n + i], refs[2 * n].at[i]) for i in range(n)]
    for copy in copies:
        copy.start()
    for copy in copies:
        copy.wait()


def write_call(*arrays):
    n = len(arrays)
    return pl.pallas_call(
        write_kernel,
        out_shape=tuple(jax.ShapeDtypeStruct(a.shape, a.dtype) for a in arrays),
        in_specs=[pl.BlockSpec(memory_space=pltpu.VMEM)] * n,
        out_specs=tuple(pl.BlockSpec(memory_space=pl.ANY) for _ in arrays),
        scratch_shapes=[pltpu.SemaphoreType.DMA((n,))],
        compiler_params=pltpu.CompilerParams(has_side_effects=True, vmem_limit_bytes=16 << 20),
        cost_estimate=pl.CostEstimate(flops=0, bytes_accessed=12 << 20, transcendentals=0),
    )(*arrays)


def on_device(inputs, cotangent, up_weight, down_weight, local_params, global_params, outer_momentum, plan, fragment_id):
    return write_call(
        *step_call(
            inputs, cotangent, up_weight, down_weight, local_params, global_params, outer_momentum, plan, fragment_id
        )
    )


def solution(mesh):
    placed = (
        P("replica", None, None),
        P("replica", "fsdp", None),
        P("replica", None, "fsdp"),
        P("replica", "fsdp", None),
        P("replica", None, "fsdp"),
        P(None, "fsdp"),
        P(None, "fsdp"),
        P(),
        P(),
    )
    return jax.shard_map(
        on_device,
        mesh=mesh,
        in_specs=placed,
        out_specs=(
            P("replica", "fsdp", None),
            P("replica", "fsdp", None),
            P("replica", None, "fsdp"),
            P("replica", "fsdp", None),
            P(None, "fsdp"),
            P(None, "fsdp"),
            P("replica", None, "fsdp"),
        ),
        check_vma=False,
    )
```

```python
import jax
import jax.numpy as jnp
from jax import lax
from jax.experimental import pallas as pl
from jax.experimental.pallas import tpu as pltpu
from jax.sharding import PartitionSpec as P

BF = jnp.bfloat16
F32 = jnp.float32
MESH = pl.DeviceIdType.MESH
HALF = 2048
NEAR = (0, 1, 3, 2)
FAR = (2, 1, 3, 0)


def dot(a, b, ca, cb):
    return lax.dot_general(a, b, (((ca,), (cb,)), ((), ())), preferred_element_type=F32)


def selected_rows(plan_ref, frag_ref):
    first, last = jnp.int32(15), jnp.int32(0)
    for layer in range(16):
        hit = plan_ref[layer] == frag_ref[0]
        first = jnp.minimum(first, jnp.where(hit, layer, 15))
        last = jnp.maximum(last, jnp.where(hit, layer, 0))
    return first, last


def step_kernel(
    x_hbm, cot_hbm, wu_hbm, wd_hbm, lp_hbm, gp_hbm, om_hbm, plan_hbm, frag_hbm,
    bo_ref, ig_ref, ug_ref, dg_ref, ng_ref, nm_ref, ml_ref,
    plan_ref, frag_ref, x_v, wu, wd, lp, gp, om, cot4, st, cotg, slope, hg, hid, pg, msg, peer_msg,
    own, sb, rb, part, r1, sp, rp,
    lsem, s1, q1, s3, q3, s4, q4, s0, q0, sr, qr, s2, q2, sx, qx,
):
    rep = lax.axis_index("replica")
    f = lax.axis_index("fsdp")
    x, y, z, c = f // 16, (f // 4) % 4, (f // 2) % 2, f % 2
    other = 1 - c
    lo = pl.multiple_of(c * HALF, HALF)
    hi = pl.multiple_of(other * HALF, HALF)
    ring = jnp.where(c == 0, x, y)
    plane = jnp.where(c == 0, y, x)

    ring_step = jnp.where(c == 0, 16, 4)
    plane_step = jnp.where(c == 0, 4, 16)
    here = plane * 4 + z * 2 + c
    peer = (rep, f + other - c)

    def on_ring(r):
        return (rep, f + (r - ring) * ring_step)

    def in_plane(k):
        return (rep, ring * ring_step + (k // 4) * plane_step + k % 4)

    def block_of(e):
        return (plane + e) % 4

    def rotate(k, fn):
        lax.fori_loop(1, 16, lambda d, _: (fn((k + d) % 16), 0)[1], 0)

    def remote(src, dst, ssem, rsem, device):
        return pltpu.make_async_remote_copy(
            src_ref=src, dst_ref=dst, send_sem=ssem, recv_sem=rsem, device_id=device, device_id_type=MESH
        )

    barrier = pltpu.get_barrier_semaphore()

    for d in range(1, 16):
        pl.semaphore_signal(barrier, inc=1, device_id=in_plane((here + d) % 16), device_id_type=MESH)
    for d in (1, 2, 3):
        pl.semaphore_signal(barrier, inc=1, device_id=on_ring((ring + d) % 4), device_id_type=MESH)
    pl.semaphore_signal(barrier, inc=1, device_id=(1 - rep, f), device_id_type=MESH)

    loads = [
        pltpu.make_async_copy(cot_hbm.at[0], cot4, lsem.at[0]),
        pltpu.make_async_copy(x_hbm.at[0], x_v, lsem.at[1]),
        pltpu.make_async_copy(wu_hbm.at[0], wu, lsem.at[2]),
        pltpu.make_async_copy(wd_hbm.at[0], wd, lsem.at[3]),
        pltpu.make_async_copy(lp_hbm.at[0], lp, lsem.at[4]),
        pltpu.make_async_copy(gp_hbm, gp, lsem.at[5]),
        pltpu.make_async_copy(om_hbm, om, lsem.at[6]),
        pltpu.make_async_copy(plan_hbm, plan_ref, lsem.at[7]),
        pltpu.make_async_copy(frag_hbm, frag_ref, lsem.at[8]),
    ]
    for k in (0, 1, 2, 3, 7, 8, 4, 5, 6):
        loads[k].start()
    pl.semaphore_wait(barrier, 19)

    loads[0].wait()
    st[here] = cot4[:, pl.ds(lo, HALF)]

    def same_core(d):
        target = ring * ring_step + block_of(NEAR[d // 2]) * plane_step + (z + d) % 2 * 2 + c
        return remote(cot4.at[:, pl.ds(lo, HALF)], st.at[here], s1.at[0], q1.at[plane], (rep, target))

    def other_core(d):
        target = (ring + NEAR[d // 2]) % 4 * ring_step + plane * plane_step + (z + d) % 2 * 2 + other
        return remote(cot4.at[:, pl.ds(hi, HALF)], st.at[ring * 4 + z * 2 + c], s1.at[0], q1.at[ring], (rep, target))

    for d in range(8):
        if d:
            same_core(d).start()
        other_core(d).start()

    loads[1].wait()
    loads[2].wait()
    slope[...] = dot(x_v[...], wu[...], 1, 0)
    u = slope[...]
    t = jnp.tanh(0.7978845608 * (u + 0.044715 * u * u * u))
    hid[...] = (0.5 * u * (1.0 + t)).astype(BF)
    slope[...] = 0.5 * (1.0 + t) + 0.5 * u * (1.0 - t * t) * 0.7978845608 * (1.0 + 3.0 * 0.044715 * u * u)

    def block0(r, q):
        return cotg.at[r, q, :, pl.ds(0, HALF)]

    def block1(r, q):
        return cotg.at[q, r, :, pl.ds(HALF, HALF)]

    def ring_copy(block, e, d):
        b = block(ring, block_of(e))
        return remote(b, b, s3.at[0], q3.at[e, d - 1], on_ring((ring + d) % 4))

    def core_copy(block, e, d):
        b = block((ring + 4 - d) % 4, block_of(e))
        return remote(b, b, s4.at[0], q4.at[0], peer)

    def per_core(fn):
        @pl.when(c == 0)
        def _():
            fn(block0)

        @pl.when(c == 1)
        def _():
            fn(block1)

    def pieces(e):
        n = 4 if e else 3
        return remote(st.at[pl.ds(0, n)], st.at[pl.ds(0, n)], s1.at[0], q1.at[block_of(e)], peer)

    for e in NEAR:
        pieces(e).wait_recv()
        q = block_of(e)
        block = jnp.concatenate([st[4 * q + i].astype(F32) for i in range(4)], axis=0).astype(BF)

        def stage2(where):
            if where is block0:
                cotg[x, q, :, 0:HALF] = block
            else:
                cotg[q, y, :, HALF:] = block
            for d in (2, 1, 3):
                ring_copy(where, e, d).start()
            core_copy(where, e, 0).start()

        per_core(stage2)

    loads[4].wait()
    loads[7].wait()
    loads[8].wait()
    i0, i1 = selected_rows(plan_ref, frag_ref)
    msg[0:1, :] = lp[pl.ds(i0, 1), :].astype(BF)
    msg[1:2, :] = lp[pl.ds(i1, 1), :].astype(BF)
    swap = remote(msg, peer_msg, sx.at[0], qx.at[0], (1 - rep, f))
    swap.start()

    def first(n, product):
        sb[n] = product(hi).astype(BF).reshape(4, 4, 16, HALF)
        for core in (0, 1):
            @pl.when(c == core)
            def _():
                for e in FAR:
                    q = (ring + e) % 4
                    src, dst = (sb.at[n, q], rb.at[n, q]) if core == 0 else (sb.at[n, :, q], rb.at[n, :, q])
                    remote(src, dst, s0.at[n], q0.at[n, e], peer).start()
        own[...] = product(lo).reshape(4, 4, 16, HALF)

    def combine(n, core, e):
        q = block_of(e)
        remote(rb.at[n, 0], rb.at[n, 0], s0.at[n], q0.at[n, e], peer).wait_recv()
        if core == 0:
            part[n, :, q] = (own[:, q] + rb[n, :, q].astype(F32)).astype(BF)
        else:
            part[n, q] = (own[q] + rb[n, q].astype(F32)).astype(BF)

    def ring_send(n, core, e):
        q = block_of(e)
        for d in (2, 1, 3):
            r = (ring + d) % 4
            src = part.at[n, r, q] if core == 0 else part.at[n, q, r]
            remote(src, r1.at[n, d - 1, q], sr.at[n], qr.at[n, e], on_ring(r)).start()

    def blocks(*acts):
        for core in (0, 1):
            @pl.when(c == core)
            def _():
                for e in FAR:
                    for act in acts:
                        act(core, e)

    def third(*sums):
        slot = c * 8 + plane * 2 + z
        for e, n in ((e, n) for e in FAR for n in sums):
            q = block_of(e)
            got = r1.at[n, :, q]
            remote(got, got, sr.at[n], qr.at[n, e], peer).wait_recv()
            mine = jnp.where(c == 0, part[n, x, q].astype(F32), part[n, q, y].astype(F32))
            v = mine + r1[n, 0, q].astype(F32) + r1[n, 1, q].astype(F32) + r1[n, 2, q].astype(F32)
            for i in range(4):
                sp[n, 4 * q + i] = v[4 * i : 4 * i + 4].astype(BF)
            for i in (2, 3, 0, 1) if e else (2, 3, 1):
                k = 4 * q + (z * 2 + c + i) % 4
                remote(sp.at[n, k], rp.at[n, slot], s2.at[n], q2.at[n], in_plane(k)).start()
        for n in sums:
            rp[n, slot] = sp[n, here]

    def third_all(n):
        return remote(sp.at[n, pl.ds(0, 15)], rp.at[n, pl.ds(0, 15)], s2.at[n], q2.at[n], peer)

    def third_done(n, out):
        third_all(n).wait_recv()
        for h in (0, 1):
            v = rp[n, 8 * h].astype(F32)
            for k in range(1, 8):
                v = v + rp[n, 8 * h + k].astype(F32)
            out[0, :, h * HALF : (h + 1) * HALF] = v.astype(BF)

    loads[3].wait()
    first(0, lambda at: dot(hid[...], wd[:, pl.ds(at, HALF)], 1, 0))
    blocks(lambda core, e: combine(0, core, e))

    def stage3(where):
        for i, e in enumerate(NEAR):
            if i == 3:
                most = cotg.at[pl.ds(0, 3), :, :, pl.ds(0, HALF)]
                remote(most, most, s3.at[0], q3.at[0, 0], peer).wait_send()
                for b in FAR:
                    ring_send(0, 0 if where is block0 else 1, b)
            for d in (2, 1, 3):
                ring_copy(where, e, d).wait_recv()
                core_copy(where, e, d).start()

    per_core(stage3)

    def half_grad(at):
        return dot(cotg[:, :, :, pl.ds(at, HALF)].reshape(256, HALF), wd[:, pl.ds(at, HALF)], 1, 1)

    hg[...] = half_grad(lo)
    theirs = cotg.at[:, :, :, pl.ds(hi, HALF)]
    remote(theirs, theirs, s4.at[0], q4.at[0], peer).wait_recv()

    pg[...] = ((hg[...] + half_grad(hi)) * slope[...]).astype(BF)
    first(1, lambda at: dot(pg[...], wu[pl.ds(at, HALF), :], 1, 1))
    blocks(lambda core, e: combine(1, core, e), lambda core, e: ring_send(1, core, e))

    dg_ref[0] = dot(hid[...], cotg[...].reshape(256, 4096), 0, 0).astype(BF)
    ug_ref[0] = dot(x_v[...], pg[...], 0, 0).astype(BF)
    third(0, 1)

    loads[5].wait()
    loads[6].wait()
    swap.wait_recv()
    for e in range(0, 16384, 2048):
        cols = slice(e, e + 2048)
        mine, g, mom = lp[:, cols], gp[:, cols], om[:, cols]
        row = lax.broadcasted_iota(jnp.int32, mine.shape, 0)
        keep = (row == i0) | (row == i1)
        theirs = peer_msg[:, cols].astype(F32)
        far = jnp.where(row == i0, theirs[0:1, :], theirs[1:2, :])
        delta = g - (mine.astype(BF).astype(F32) + far) / 2
        momentum = 0.9 * mom + delta
        ng = jnp.where(keep, g - 0.7 * (delta + 0.9 * momentum), g)
        nm_ref[:, cols] = jnp.where(keep, momentum, mom)
        ng_ref[:, cols] = ng
        ml_ref[0, :, cols] = jnp.where(keep, 0.5 * mine + 0.5 * ng, mine)

    third_done(0, bo_ref)
    third_done(1, ig_ref)

    swap.wait_send()
    remote(st.at[pl.ds(0, 15)], st.at[pl.ds(0, 15)], s1.at[0], q1.at[0], peer).wait_send()
    half = cotg.at[:, :, :, pl.ds(0, HALF)]
    remote(half, half, s4.at[0], q4.at[0], peer).wait_send()
    for n in (0, 1):
        remote(sb.at[n], rb.at[n], s0.at[n], q0.at[n, 0], peer).wait_send()
        remote(r1.at[n], r1.at[n], sr.at[n], qr.at[n, 0], peer).wait_send()
        third_all(n).wait_send()


def step_call(x, cot, wu, wd, lp, gp, om, plan, frag):
    hbm = pl.BlockSpec(memory_space=pl.ANY)
    smem = pl.BlockSpec(memory_space=pltpu.SMEM)
    vmem = pl.BlockSpec(memory_space=pltpu.VMEM)
    dma = pltpu.SemaphoreType.DMA
    return pl.pallas_call(
        step_kernel,
        out_shape=(
            pltpu.VMEM((1, 4, 4096), BF),
            pltpu.VMEM((1, 4, 4096), BF),
            pltpu.VMEM((1, 4096, 512), BF),
            pltpu.VMEM((1, 512, 4096), BF),
            pltpu.VMEM((16, 16384), F32),
            pltpu.VMEM((16, 16384), F32),
            pltpu.VMEM((1, 16, 16384), F32),
        ),
        in_specs=[hbm] * 9,
        out_specs=(vmem,) * 7,
        scratch_shapes=[
            pltpu.SMEM((16,), jnp.int32),
            pltpu.SMEM((1,), jnp.int32),
            pltpu.VMEM((256, 4096), BF),
            pltpu.VMEM((4096, 512), BF),
            pltpu.VMEM((512, 4096), BF),
            pltpu.VMEM((16, 16384), F32),
            pltpu.VMEM((16, 16384), F32),
            pltpu.VMEM((16, 16384), F32),
            pltpu.VMEM((4, 4096), BF),
            pltpu.VMEM((16, 4, HALF), BF),
            pltpu.VMEM((4, 4, 16, 4096), BF),
            pltpu.VMEM((256, 512), F32),
            pltpu.VMEM((256, 512), F32),
            pltpu.VMEM((256, 512), BF),
            pltpu.VMEM((256, 512), BF),
            pltpu.VMEM((2, 16384), BF),
            pltpu.VMEM((2, 16384), BF),
            pltpu.VMEM((4, 4, 16, HALF), F32),
            pltpu.VMEM((2, 4, 4, 16, HALF), BF),
            pltpu.VMEM((2, 4, 4, 16, HALF), BF),
            pltpu.VMEM((2, 4, 4, 16, HALF), BF),
            pltpu.VMEM((2, 3, 4, 16, HALF), BF),
            pltpu.VMEM((2, 16, 4, HALF), BF),
            pltpu.VMEM((2, 16, 4, HALF), BF),
            dma((9,)),
            dma((1,)), dma((4,)),
            dma((1,)), dma((4, 3)),
            dma((1,)), dma((1,)),
            dma((2,)), dma((2, 4)),
            dma((2,)), dma((2, 4)),
            dma((2,)), dma((2,)),
            dma((1,)), dma((1,)),
        ],
        compiler_params=pltpu.CompilerParams(collective_id=1, has_side_effects=True, vmem_limit_bytes=46 << 20),
        cost_estimate=pl.CostEstimate(flops=6 * 2 * 256 * 4096 * 512, bytes_accessed=14 << 20, transcendentals=1 << 17),
    )(x, cot, wu, wd, lp, gp, om, plan, frag)


def write_kernel(*refs):
    n = len(refs) // 2
    copies = [pltpu.make_async_copy(refs[i], refs[n + i], refs[2 * n].at[i]) for i in range(n)]
    for copy in copies:
        copy.start()
    for copy in copies:
        copy.wait()


def write_call(*arrays):
    n = len(arrays)
    return pl.pallas_call(
        write_kernel,
        out_shape=tuple(jax.ShapeDtypeStruct(a.shape, a.dtype) for a in arrays),
        in_specs=[pl.BlockSpec(memory_space=pltpu.VMEM)] * n,
        out_specs=tuple(pl.BlockSpec(memory_space=pl.ANY) for _ in arrays),
        scratch_shapes=[pltpu.SemaphoreType.DMA((n,))],
        compiler_params=pltpu.CompilerParams(has_side_effects=True, vmem_limit_bytes=16 << 20),
        cost_estimate=pl.CostEstimate(flops=0, bytes_accessed=12 << 20, transcendentals=0),
    )(*arrays)


def on_device(inputs, cotangent, up_weight, down_weight, local_params, global_params, outer_momentum, plan, fragment_id):
    return write_call(
        *step_call(
            inputs, cotangent, up_weight, down_weight, local_params, global_params, outer_momentum, plan, fragment_id
        )
    )


def solution(mesh):
    placed = (
        P("replica", None, None),
        P("replica", "fsdp", None),
        P("replica", None, "fsdp"),
        P("replica", "fsdp", None),
        P("replica", None, "fsdp"),
        P(None, "fsdp"),
        P(None, "fsdp"),
        P(),
        P(),
    )
    return jax.shard_map(
        on_device,
        mesh=mesh,
        in_specs=placed,
        out_specs=(
            P("replica", "fsdp", None),
            P("replica", "fsdp", None),
            P("replica", None, "fsdp"),
            P("replica", "fsdp", None),
            P(None, "fsdp"),
            P(None, "fsdp"),
            P("replica", None, "fsdp"),
        ),
        check_vma=False,
    )
```
